128 devices in a mesh: row: 16 (over x, z), col: 8 (over y, core).
Axes of the slice: x: 4, y: 4, z: 4, core: 2. Of those that a mesh axis runs over, the one named last changes fastest.
Arguments:
- currents: bfloat16 [256, 128, 512], P('row', 'col'), may hold values from -6 to 6
- counts: int32 [256, 128], P('row', 'col'), may hold values from 0 to 16
- radiate: bfloat16 [512, 1024], replicated, may hold values from -0.25 to 0.25
- receive: bfloat16 [1024, 512], replicated, may hold values from -0.1875 to 0.1875
- near_blocks: bfloat16 [9, 512, 512], replicated, may hold values from -0.09375 to 0.09375
- translate: float32 [4, 49, 1024], replicated, may hold values from -0.84 to 0.84
- shift: float32 [3, 4, 1024], replicated, may hold values from -3 to 3
Outputs:
- field: bfloat16 [256, 128, 512], P('row', 'col')
The draws below stay inside these ranges and needn't reach their ends.
Inputs may be any that keep to these rules, and one draw needn't show every extreme that they name: `counts`: atoms present in each leaf box; they occupy its first slots.
All inputs are finite; a program needn't handle non-finite values.
Results may differ from the reference program's by a relative error of at most 0.017.
Values may be sent and summed in bfloat16 or wider, within the bound.
No kernel may reach another device: no remote copies, remote signals or barrier semaphores. Data moves between devices by JAX's collectives and lax.ppermute only.
A program may use at most 192 MiB of HBM per device.

```python
import jax
import jax.numpy as jnp
from jax import lax

U = 16
SLOTS = 16
LEVELS = 4
W = 512
P_SIZE = 1024
NBX = 256
NBY = 128


def plant(result, key, least, high):
    extent = result.shape
    spot = [jax.random.randint(jax.random.fold_in(key, axis), (), 0, extent[axis]) for axis in range(len(extent))]
    result = result.at[tuple(spot)].set(least)
    longest = extent.index(max(extent))
    spot[longest] = (spot[longest] + 1) % extent[longest]
    return result.at[tuple(spot)].set(high)


def block_scale(key, shape, pieces, least, high):
    factor_of, own = 1.0, jax.random.fold_in(key, 6)
    for dim, parts in pieces:
        draws = jnp.exp(jax.random.uniform(jax.random.fold_in(own, dim), (parts,), jnp.float32, least / len(pieces), high / len(pieces)))
        factor_of = factor_of * jnp.repeat(draws, shape[dim] // parts).reshape([-1 if axis == dim else 1 for axis in range(len(shape))])
    return factor_of


def gaussian(stream_key, dims, scale, limit, cuts=(), kind=jnp.bfloat16):
    factor_of = block_scale(stream_key, dims, cuts, -0.22, 0.18) if cuts else 1.0
    array = jax.random.normal(stream_key, dims, jnp.float32) * scale * factor_of
    return jnp.minimum(jnp.maximum(array, -limit), limit).astype(kind)


def setup_inputs(seed: int = 0) -> dict:
    seeds = jax.random.split(jax.random.key(seed), 8)
    currents = gaussian(seeds[0], (NBX, NBY, W), 1.0, 6.0, ((0, 16), (1, 8)))
    counts = plant(jax.random.randint(seeds[1], (NBX, NBY), 0, SLOTS + 1), jax.random.fold_in(seeds[1], 1), 0, SLOTS).astype(jnp.int32)
    radiate = gaussian(seeds[2], (W, P_SIZE), W ** -0.5, 0.25)
    receive = gaussian(seeds[3], (P_SIZE, W), P_SIZE ** -0.5, 0.1875)
    near_blocks = gaussian(seeds[4], (9, W, W), (9 * W) ** -0.5, 0.09375)
    translate = gaussian(seeds[5], (LEVELS, 49, P_SIZE), 0.14, 0.84, (), jnp.float32)
    shift = gaussian(seeds[6], (LEVELS - 1, 4, P_SIZE), 0.5, 3.0, (), jnp.float32)
    return {"currents": currents, "counts": counts, "radiate": radiate, "receive": receive, "near_blocks": near_blocks, "translate": translate, "shift": shift}


def rotate(factors, pattern):
    samples = pattern.shape[-1] // 2
    t_re = factors[..., :samples]
    t_im = factors[..., samples:]
    p_re = pattern[..., :samples]
    p_im = pattern[..., samples:]
    return jnp.concatenate([t_re * p_re - t_im * p_im, t_re * p_im + t_im * p_re], axis=-1)


def rotate_back(factors, pattern):
    samples = pattern.shape[-1] // 2
    t_re = factors[..., :samples]
    t_im = factors[..., samples:]
    p_re = pattern[..., :samples]
    p_im = pattern[..., samples:]
    return jnp.concatenate([t_re * p_re + t_im * p_im, t_re * p_im - t_im * p_re], axis=-1)


def ascend(children, factors):
    size_x, size_y, last_dim = children.shape
    grouped = children.astype(jnp.float32).reshape(size_x // 2, 2, size_y // 2, 2, last_dim)
    summed = jnp.zeros((size_x // 2, size_y // 2, last_dim), jnp.float32)
    for bit_x in range(2):
        for bit_y in range(2):
            summed = summed + rotate(factors[2 * bit_x + bit_y], grouped[:, bit_x, :, bit_y])
    return summed.astype(jnp.bfloat16)


def descend(parent, factors):
    size_x, size_y, last_dim = parent.shape
    stacked = []
    for bit_x in range(2):
        siblings = [rotate_back(factors[2 * bit_x + bit_y], parent) for bit_y in range(2)]
        stacked.append(jnp.stack(siblings, axis=2))
    return jnp.stack(stacked, axis=1).reshape(2 * size_x, 2 * size_y, last_dim)


def far_field(padded, factors, size_x, size_y):
    index_x = jnp.arange(size_x, dtype=jnp.int32)
    index_y = jnp.arange(size_y, dtype=jnp.int32)
    summed = jnp.zeros((size_x, size_y, padded.shape[-1]), jnp.float32)
    for step_x in range(-3, 4):
        keep_x = jnp.abs((index_x + step_x) // 2 - index_x // 2) <= 1
        for step_y in range(-3, 4):
            if max(abs(step_x), abs(step_y)) < 2:
                continue
            keep_y = jnp.abs((index_y + step_y) // 2 - index_y // 2) <= 1
            keep_both = keep_x[:, None] & keep_y[None, :]
            source = padded[3 + step_x:3 + step_x + size_x, 3 + step_y:3 + step_y + size_y].astype(jnp.float32)
            contrib = rotate(factors[(step_x + 3) * 7 + step_y + 3], source)
            summed = summed + jnp.where(keep_both[:, :, None], contrib, 0.0)
    return summed


def reference(currents, counts, radiate, receive, near_blocks, translate, shift):
    size_x, size_y, unknowns = currents.shape
    slot_of = lax.broadcasted_iota(jnp.int32, (1, 1, unknowns), 2) // (2 * U)
    occupied = slot_of < counts[:, :, None]
    masked = jnp.where(occupied, currents, jnp.zeros_like(currents))
    padded_near = jnp.pad(masked, ((1, 1), (1, 1), (0, 0)))
    near_sum = jnp.zeros((size_x * size_y, unknowns), jnp.float32)
    for step_x in range(-1, 2):
        for step_y in range(-1, 2):
            source = padded_near[1 + step_x:1 + step_x + size_x, 1 + step_y:1 + step_y + size_y].reshape(size_x * size_y, unknowns)
            near_sum = near_sum + jnp.dot(source, near_blocks[(step_x + 1) * 3 + step_y + 1], preferred_element_type=jnp.float32)
    flat_rows = masked.reshape(size_x * size_y, unknowns)
    leaf_pattern = jnp.dot(flat_rows, radiate, preferred_element_type=jnp.float32).astype(jnp.bfloat16)
    pyramid = [leaf_pattern.reshape(size_x, size_y, P_SIZE)]
    for level_no in range(1, LEVELS):
        pyramid.append(ascend(pyramid[-1], shift[level_no - 1]))
    top_pattern = pyramid[LEVELS - 1]
    incoming = far_field(jnp.pad(top_pattern, ((3, 3), (3, 3), (0, 0))), translate[LEVELS - 1], top_pattern.shape[0], top_pattern.shape[1])
    for level_no in range(LEVELS - 2, -1, -1):
        current = pyramid[level_no]
        far_sum = far_field(jnp.pad(current, ((3, 3), (3, 3), (0, 0))), translate[level_no], current.shape[0], current.shape[1])
        incoming = far_sum + descend(incoming, shift[level_no])
    incoming_half = incoming.astype(jnp.bfloat16).reshape(size_x * size_y, P_SIZE)
    back_sum = jnp.dot(incoming_half, receive, preferred_element_type=jnp.float32)
    field = (near_sum + back_sum).reshape(size_x, size_y, unknowns)
    return jnp.where(occupied, field, 0.0).astype(jnp.bfloat16)
```

```python
import functools

import jax
import jax.numpy as jnp
from jax import lax
from jax.experimental import pallas as pl
from jax.experimental.pallas import tpu as pltpu
from jax.sharding import PartitionSpec as P

U = 16
INTERPRET = False
F32 = jnp.float32
BF16 = jnp.bfloat16
N0 = 16
ROW0 = 32
ROWS = 24
SX = 72
SY = 48
OFFS = [(dx, dy) for dx in range(-3, 4) for dy in range(-3, 4) if max(abs(dx), abs(dy)) >= 2]


def lanes(c):
    return slice(c * 128, (c + 1) * 128)


def occupied_rows(cnt_ref, x):
    row = cnt_ref[x : x + 1, :].astype(F32)
    one = lax.broadcasted_iota(jnp.int32, (N0, N0), 0) == lax.broadcasted_iota(jnp.int32, (N0, N0), 1)
    count = jnp.sum(jnp.where(one, jnp.broadcast_to(row, (N0, N0)), 0.0), axis=1, keepdims=True)
    lane = lax.broadcasted_iota(jnp.int32, (N0, 512), 1).astype(F32)
    return lane < count * float(2 * U)


def swap_perm(count, odd):
    pairs = [(i, i + 1) for i in range(odd, count - 1, 2)]
    if odd:
        pairs.append((count - 1, 0))
    return pairs + [(b, a) for a, b in pairs]


def upward(cur, cnt, rad, shf, msk, p0, p1, p2, p3, m_even, m_odd, c0, f0, me, mo):
    even = (lax.axis_index("col") % 2) == 0
    for x in range(N0):
        kept = jnp.where(occupied_rows(cnt, x), cur[x].astype(F32), 0.0)
        msk[x] = kept.astype(BF16)
        for c in range(4):
            c0[c, x * 16 : (x + 1) * 16, :] = kept[:, lanes(c)]
    lhs = msk[...].reshape(N0 * N0, 512)
    for n in range(4):
        out = jnp.dot(lhs, rad[:, n * 256 : (n + 1) * 256], preferred_element_type=F32).astype(BF16)
        for h in range(2):
            p0[2 * n + h] = out[:, lanes(h)]
            f0[2 * n + h] = out[:, lanes(h)].astype(F32)
    source, rows = f0, 16
    for level, (dest, size) in enumerate(((p1, 8), (p2, 4), (p3, 2))):
        for i in range(size):
            for c in range(4):
                re = im = None
                for a in range(2):
                    for b in range(2):
                        at = pl.ds((2 * i + a) * rows + b, size, stride=2)
                        s_re = source[c, at, :]
                        s_im = source[4 + c, at, :]
                        t_re = shf[level, 2 * a + b : 2 * a + b + 1, lanes(c)]
                        t_im = shf[level, 2 * a + b : 2 * a + b + 1, lanes(4 + c)]
                        q_re = t_re * s_re - t_im * s_im
                        q_im = t_re * s_im + t_im * s_re
                        re = q_re if re is None else re + q_re
                        im = q_im if im is None else im + q_im
                dest[c, i * 8 : i * 8 + size, :] = re.astype(BF16).astype(F32)
                dest[4 + c, i * 8 : i * 8 + size, :] = im.astype(BF16).astype(F32)
        source, rows = dest, 8

    def put(c, at, lo, hi):
        me[c, at, :] = jnp.where(even, hi, lo)
        mo[c, at, :] = jnp.where(even, lo, hi)

    for r in range(2):
        for c in range(4):
            lo = c0[c, pl.ds(r, 16, stride=16), :]
            hi = c0[c, pl.ds(14 + r, 16, stride=16), :]
            for h in range(2):
                put(c + 4 * h, pl.ds(r, 8, stride=2), lo[8 * h : 8 * h + 8], hi[8 * h : 8 * h + 8])
        for c in range(8):
            put(c, pl.ds(16 + r, 8, stride=2), p1[c, pl.ds(r, 8, stride=8), :], p1[c, pl.ds(6 + r, 8, stride=8), :])
            put(c, pl.ds(32 + r, 4, stride=2), p2[c, pl.ds(r, 4, stride=8), :], p2[c, pl.ds(2 + r, 4, stride=8), :])
            both = p3[c, pl.ds(r, 2, stride=8), :]
            put(c, pl.ds(40 + r, 2, stride=2), both, both)
    for c in range(8):
        me[c, 44:48, :] = jnp.zeros((4, 128), F32)
        mo[c, 44:48, :] = jnp.zeros((4, 128), F32)
        m_even[c] = me[c].astype(BF16)
        m_odd[c] = mo[c].astype(BF16)


def received(axis, r_even, r_odd, lo, hi):
    me = lax.axis_index(axis)
    last = lax.axis_size(axis) - 1
    even = (me % 2) == 0
    for c in range(8):
        from_even = r_even[c].astype(F32)
        from_odd = r_odd[c].astype(F32)
        lo[c] = jnp.where(me == 0, 0.0, jnp.where(even, from_odd, from_even))
        hi[c] = jnp.where(me == last, 0.0, jnp.where(even, from_even, from_odd))


def strips(r_even, r_odd, msk, p1, p2, p3, x_even, x_odd, ylo, yhi, mlo, mhi):
    received("col", r_even, r_odd, ylo, yhi)
    even = (lax.axis_index("row") % 2) == 0
    for dest, first in ((mlo, 0), (mhi, 1)):
        for xr in range(2):
            x = 14 * first + xr
            kept = msk[x].astype(F32)
            for c in range(4):
                dest[4 * xr + c, 2:18, :] = kept[:, lanes(c)]
                at = slice(2 * (x % 8), 2 * (x % 8) + 2)
                dest[4 * xr + c, 0:2, :] = ylo[c + 4 * (x // 8), at, :]
                dest[4 * xr + c, 18:20, :] = yhi[c + 4 * (x // 8), at, :]
            for c in range(8):
                for level_ref, size, base, inside in ((p1, 8, 32, 16), (p2, 4, 56, 32), (p3, 2, 20, 40)):
                    x = (size - 2) * first + xr
                    at = base + (size + 4) * xr
                    dest[c, at + 2 : at + 2 + size, :] = level_ref[c, x * 8 : x * 8 + size, :]
                    dest[c, at : at + 2, :] = ylo[c, inside + 2 * x : inside + 2 * x + 2, :]
                    dest[c, at + 2 + size : at + 4 + size, :] = yhi[c, inside + 2 * x : inside + 2 * x + 2, :]
    for c in range(8):
        lo = mlo[c]
        hi = mhi[c]
        x_even[c] = jnp.where(even, hi, lo).astype(BF16)
        x_odd[c] = jnp.where(even, lo, hi).astype(BF16)


def twice(ref, m, at):
    return jnp.concatenate([ref[2 * m, at, :], ref[2 * m + 1, at, :]], axis=0)


def parity_rows():
    return (lax.broadcasted_iota(jnp.int32, (16, 128), 0) % 2) == 0


def factor_tile(tr, level, offset, m):
    dx, dy = offset
    row = (dx + 3) * 7 + dy + 3
    low = jnp.broadcast_to(tr[level, row : row + 1, lanes(2 * m)], (8, 128))
    high = jnp.broadcast_to(tr[level, row : row + 1, lanes(2 * m + 1)], (8, 128))
    return jnp.concatenate([low, high], axis=0)


def add_product(part, factor, value):
    t_re, t_im = factor
    v_re, v_im = value
    re = t_re * v_re - t_im * v_im
    im = t_re * v_im + t_im * v_re
    return (re, im) if part is None else (part[0] + re, part[1] + im)


def add_part(total, part):
    re, im = part[0].astype(F32), part[1].astype(F32)
    return (re, im) if total is None else (total[0] + re, total[1] + im)


def leaf_far(sk, tt, inc, first, last):
    for m in range(2):

        def body(i, carry):
            total = {}
            for pair in range(3):
                part = {}
                for xs in (2 * pair, 2 * pair + 1):
                    for k in range(6):
                        if xs in (2, 3) and k in (2, 3):
                            continue
                        value = (sk[k, 2 * i + xs, m], sk[k, 2 * i + xs, 2 + m])
                        for a in range(2):
                            for b in range(2):
                                offset = (xs - 2 - a, k - 2 - b)
                                if offset not in OFFS:
                                    continue
                                o = OFFS.index(offset)
                                part[a, b] = add_product(part.get((a, b)), (tt[o, m], tt[o, 2 + m]), value)
                for key in part:
                    total[key] = add_part(total.get(key), part[key])
            for (a, b), sums in total.items():
                for q in range(2):
                    for h in range(2):
                        inc[4 * q + 2 * m + h, pl.ds((2 * i + a) * 16 + b, 8, stride=2), :] = sums[q][8 * h : 8 * h + 8]
            return carry

        lax.fori_loop(first, last, body, 0)


def slots_of(dx):
    full = [(k, k - 2, k - 3) for k in range(6)]
    return full if abs(dx) >= 2 else [full[0], full[5], (6, 2, -2)]


SLOTS = [(dx, slot) for dx in range(-3, 4) for slot in slots_of(dx)]


def level_tables(tr, level, ts):
    rows = parity_rows()
    for s, (dx, (_, dy_even, dy_odd)) in enumerate(SLOTS):
        for m in range(4):
            tile = jnp.where(rows, factor_tile(tr, level, (dx, dy_even), m), factor_tile(tr, level, (dx, dy_odd), m))
            ts[s, m] = tile.astype(BF16)


def level_sources(fx, sk, xes):
    rows = parity_rows()
    for xe in xes:
        for m in range(4):
            views = [twice(fx, m, slice(xe * ROWS + 6 + d, xe * ROWS + 14 + d)) for d in range(-1, 6)]
            for k in range(6):
                sk[k, xe, m] = jnp.where(rows, views[k + 1], views[k]).astype(BF16)
            sk[6, xe, m] = jnp.where(rows, views[5], views[1]).astype(BF16)


def level_far(sk, ts, inc, size):
    for i in range(size // 2):
        for a in range(2):
            for m in range(2):
                total = None
                for pair in range(3):
                    part = None
                    for xs in (2 * pair, 2 * pair + 1):
                        dx = xs - 2 - a
                        for slot in slots_of(dx):
                            s = SLOTS.index((dx, slot))
                            value = (sk[slot[0], 2 * i + xs, m], sk[slot[0], 2 * i + xs, 2 + m])
                            part = add_product(part, (ts[s, m], ts[s, 2 + m]), value)
                    total = add_part(total, part)
                x = 2 * i + a
                for q in range(2):
                    for h in range(2):
                        inc[4 * q + 2 * m + h, x * 8 : x * 8 + size, :] = total[q][8 * h : 8 * h + size]


def add_parent(inc, parent, shf, level, size, rows):
    half = size // 2
    for x in range(size):
        for b in range(2):
            row = 2 * (x % 2) + b
            at = pl.ds(x * rows + b, half, stride=2)
            for c in range(4):
                q_re = parent[c, (x // 2) * 8 : (x // 2) * 8 + half, :]
                q_im = parent[4 + c, (x // 2) * 8 : (x // 2) * 8 + half, :]
                t_re = shf[level, row : row + 1, lanes(c)]
                t_im = shf[level, row : row + 1, lanes(4 + c)]
                inc[c, at, :] = inc[c, at, :] + (t_re * q_re + t_im * q_im)
                inc[4 + c, at, :] = inc[4 + c, at, :] + (t_re * q_im - t_im * q_re)


def downward(
    cnt, msk, p0, p1, p2, p3, r_even, r_odd, x_even, x_odd, rad, rec, near, tr, shf, field,
    ylo, yhi, xlo, xhi, cx, ln, f0, res, sk0, tt, f1, f2, f3, sk1, sk2, sk3, ts, inc0, inc1, inc2, inc3, half,
):
    received("col", r_even, r_odd, ylo, yhi)
    received("row", x_even, x_odd, xlo, xhi)
    for x in range(N0):
        kept = msk[x].astype(F32)
        base = (x + 2) * ROW0
        at = slice(2 * (x % 8), 2 * (x % 8) + 2)
        for c in range(4):
            cx[c, base + 8 : base + 24, :] = kept[:, lanes(c)]
            cx[c, base + 6 : base + 8, :] = ylo[c + 4 * (x // 8), at, :]
            cx[c, base + 24 : base + 26, :] = yhi[c + 4 * (x // 8), at, :]
    for src, xe in ((xlo, 0), (xhi, 18)):
        for xr in range(2):
            for c in range(4):
                cx[c, (xe + xr) * ROW0 + 6 : (xe + xr) * ROW0 + 26, :] = src[4 * xr + c, 0:20, :]
    for xi in range(18):
        for dy in range(-1, 2):
            for c in range(4):
                at = (xi + 1) * ROW0 + 8 + dy
                ln[xi, :, (dy + 1) * 512 + c * 128 : (dy + 1) * 512 + (c + 1) * 128] = cx[c, at : at + 16, :].astype(BF16)
    near_sum = None
    for dx in range(3):
        left = ln[dx : dx + 16].reshape(N0 * N0, 1536)
        for dy in range(3):
            term = jnp.dot(left[:, dy * 512 : (dy + 1) * 512], near[3 * dx + dy], preferred_element_type=F32)
            near_sum = term if near_sum is None else near_sum + term
    sides = [jnp.concatenate([src[4 * h + c, 0:16, :] for c in range(4)], axis=1) for src in (ylo, yhi) for h in range(2)]
    for xe in (0, 1, 18, 19):
        sides.append(jnp.concatenate([cx[c, xe * ROW0 : (xe + 1) * ROW0, :] for c in range(4)], axis=1))
    halo = jnp.dot(jnp.concatenate(sides, axis=0).astype(BF16), rad[...], preferred_element_type=F32)
    halo = halo.astype(BF16).astype(F32)
    for c in range(8):
        res[c] = halo[0:64, lanes(c)]
        for n, xe in enumerate((0, 1, 18, 19)):
            f0[c, xe * ROW0 : (xe + 1) * ROW0, :] = halo[64 + 32 * n : 96 + 32 * n, lanes(c)]
        for x in range(N0):
            base = (x + 2) * ROW0
            at = 16 * (x // 8) + 2 * (x % 8)
            f0[c, base + 8 : base + 24, :] = p0[c, x * 16 : (x + 1) * 16, :].astype(F32)
            f0[c, base + 6 : base + 8, :] = res[c, at : at + 2, :]
            f0[c, base + 24 : base + 26, :] = res[c, 32 + at : 34 + at, :]
    for xe in range(20):
        for k in range(6):
            for m in range(4):
                sk0[k, xe, m] = twice(f0, m, pl.ds(xe * ROW0 + 6 + k, 8, stride=2)).astype(BF16)
    for o, offset in enumerate(OFFS):
        for m in range(4):
            tt[o, m] = factor_tile(tr, 0, offset, m).astype(BF16)
    leaf_far(sk0, tt, inc0, 0, 8)

    above = ((f1, sk1, inc1, p1, 8, 32, 16), (f2, sk2, inc2, p2, 4, 56, 32), (f3, sk3, inc3, p3, 2, 20, 40))
    for level, (fx, sk, inc, own, size, x_base, y_base) in enumerate(above, 1):
        for c in range(8):
            for x in range(size):
                base = (x + 2) * ROWS
                fx[c, base + 8 : base + 8 + size, :] = own[c, x * 8 : x * 8 + size, :]
                fx[c, base + 6 : base + 8, :] = ylo[c, y_base + 2 * x : y_base + 2 * x + 2, :]
                fx[c, base + 8 + size : base + 10 + size, :] = yhi[c, y_base + 2 * x : y_base + 2 * x + 2, :]
            for src, xe in ((xlo, 0), (xhi, size + 2)):
                for xr in range(2):
                    at = x_base + (size + 4) * xr
                    fx[c, (xe + xr) * ROWS + 6 : (xe + xr) * ROWS + 10 + size, :] = src[c, at : at + size + 4, :]
        level_tables(tr, level, ts)
        level_sources(fx, sk, range(size + 4))
        level_far(sk, ts, inc, size)
    add_parent(inc2, inc3, shf, 2, 4, 8)
    add_parent(inc1, inc2, shf, 1, 8, 8)
    add_parent(inc0, inc1, shf, 0, 16, 16)
    for c in range(8):
        half[:, lanes(c)] = inc0[c].astype(BF16)
    total = near_sum + jnp.dot(half[...], rec[...], preferred_element_type=F32)
    for x in range(N0):
        field[x] = jnp.where(occupied_rows(cnt, x), total[x * 16 : (x + 1) * 16], 0.0).astype(BF16)


def call(kernel, outs, scratch, *args):
    return pl.pallas_call(
        kernel,
        out_shape=outs,
        scratch_shapes=scratch,
        compiler_params=pltpu.CompilerParams(vmem_limit_bytes=56 * 1024 * 1024),
        interpret=INTERPRET,
    )(*args)


def shape(dims, kind):
    return jax.ShapeDtypeStruct(dims, kind)


def swap(value, axis, odd):
    return lax.ppermute(value, axis, swap_perm(lax.axis_size(axis), odd))


def shards(currents, counts, radiate, receive, near_blocks, translate, shift):
    mem = pltpu.VMEM
    masked, p0, p1, p2, p3, m_even, m_odd = call(
        upward,
        [
            shape((16, 16, 512), BF16),
            shape((8, 256, 128), BF16),
            shape((8, 64, 128), F32),
            shape((8, 32, 128), F32),
            shape((8, 16, 128), F32),
            shape((8, SY, 128), BF16),
            shape((8, SY, 128), BF16),
        ],
        [mem((4, 256, 128), F32), mem((8, 256, 128), F32), mem((8, SY, 128), F32), mem((8, SY, 128), F32)],
        currents, counts, radiate, shift,
    )
    r_even = swap(m_even, "col", 0)
    r_odd = swap(m_odd, "col", 1)
    s_even, s_odd = call(
        strips,
        [shape((8, SX, 128), BF16)] * 2,
        [mem((8, SY, 128), F32)] * 2 + [mem((8, SX, 128), F32)] * 2,
        r_even, r_odd, masked, p1, p2, p3,
    )
    x_even = swap(s_even, "row", 0)
    x_odd = swap(s_odd, "row", 1)
    return call(
        downward,
        shape((16, 16, 512), BF16),
        [
            mem((8, SY, 128), F32), mem((8, SY, 128), F32), mem((8, SX, 128), F32), mem((8, SX, 128), F32),
            mem((4, 20 * ROW0, 128), F32), mem((18, 16, 1536), BF16),
            mem((8, 20 * ROW0, 128), F32), mem((8, 64, 128), F32),
            mem((6, 20, 4, 16, 128), BF16), mem((40, 4, 16, 128), BF16),
            mem((8, 12 * ROWS, 128), F32), mem((8, 8 * ROWS, 128), F32), mem((8, 6 * ROWS, 128), F32),
            mem((7, 12, 4, 16, 128), BF16), mem((7, 8, 4, 16, 128), BF16), mem((7, 6, 4, 16, 128), BF16),
            mem((33, 4, 16, 128), BF16),
            mem((8, 256, 128), F32), mem((8, 64, 128), F32), mem((8, 32, 128), F32), mem((8, 16, 128), F32),
            mem((256, 1024), BF16),
        ],
        counts, masked, p0, p1, p2, p3, r_even, r_odd, x_even, x_odd, radiate, receive, near_blocks, translate, shift,
    )


def solution(mesh):
    return jax.shard_map(
        shards,
        mesh=mesh,
        in_specs=(P("row", "col", None), P("row", "col"), P(), P(), P(), P(), P()),
        out_specs=P("row", "col", None),
        check_vma=False,
    )
```

```python
import jax
import jax.numpy as jnp
from jax import lax
from jax.experimental import pallas as pl
from jax.experimental.pallas import tpu as pltpu
from jax.sharding import PartitionSpec as P

U = 16
INTERPRET = False
F32 = jnp.float32
BF16 = jnp.bfloat16
N0 = 16
ROW0 = 32
ROWS = 24
SX = 72
SY = 48
FIRST = 8


def far(dx, dy):
    return max(abs(dx), abs(dy)) >= 2 and max(abs(dx), abs(dy)) <= 3


def lanes(c):
    return slice(c * 128, (c + 1) * 128)


def factors(ts, level, dx, dy, c):
    row = (dx + 3) * 7 + dy + 3
    return [ts[row, level : level + 1, lanes(4 * n + c)] for n in range(3)]


def values(ref, c, at):
    return [ref[4 * n + c, at, :] for n in range(3)]


def occupied_rows(cnt_ref, x):
    row = cnt_ref[x : x + 1, :].astype(F32)
    one = lax.broadcasted_iota(jnp.int32, (N0, N0), 0) == lax.broadcasted_iota(jnp.int32, (N0, N0), 1)
    count = jnp.sum(jnp.where(one, jnp.broadcast_to(row, (N0, N0)), 0.0), axis=1, keepdims=True)
    lane = lax.broadcasted_iota(jnp.int32, (N0, 512), 1).astype(F32)
    return lane < count * float(2 * U)


def swap_perm(axis, odd):
    size = (lax.axis_size("row"), lax.axis_size("col"))
    which = ("row", "col").index(axis)
    perm = []
    for row in range(size[0]):
        for col in range(size[1]):
            at = [row, col]
            to = at[which] + (1 if at[which] % 2 == odd else -1)
            if 0 <= to < size[which]:
                at[which] = to
            else:
                at[1 - which] ^= 1
            perm.append((row * size[1] + col, at[0] * size[1] + at[1]))
    return perm


def add_product(acc, factor, value):
    terms = (factor[0] * value[2], factor[1] * value[0], factor[2] * value[1])
    return terms if acc is None else tuple(old + term for old, term in zip(acc, terms))


def complex_sum(acc):
    return acc[0] - acc[2], acc[0] + acc[1]


def opening(out):
    out[...] = jnp.zeros((8, 128), F32)


def upward(first, cur, cnt, rad, shf, msk, f0, p1, p2, p3, m_even, m_odd, c0, me, mo):
    even = (lax.axis_index("col") % 2) == 0
    for x in range(N0):
        kept = jnp.where(occupied_rows(cnt, x), cur[x].astype(F32), 0.0)
        msk[x] = kept.astype(BF16)
        for c in range(4):
            c0[c, x * 16 : (x + 1) * 16, :] = kept[:, lanes(c)]
    lhs = msk[...].reshape(N0 * N0, 512)
    zero = jnp.zeros((8, 128), F32)
    for m in range(2):
        re, im = [
            jnp.dot(lhs, rad[:, n : n + 256], preferred_element_type=F32).astype(BF16).astype(F32)
            for n in (256 * m, 512 + 256 * m)
        ]
        for n, out in enumerate((re, im, re + im)):
            for h in range(2):
                for x in range(N0):
                    base = (x + 2) * ROW0
                    c = 4 * n + 2 * m + h
                    f0[c, base : base + 8, :] = zero
                    f0[c, base + 8 : base + 24, :] = out[x * 16 : (x + 1) * 16, lanes(h)]
                    f0[c, base + 24 : base + 32, :] = zero
    for level, (dest, size) in enumerate(((p1, 8), (p2, 4), (p3, 2))):
        for i in range(size):
            for c in range(4):
                acc = None
                for a in range(2):
                    for b in range(2):
                        if level == 0:
                            at = pl.ds((2 * i + a + 2) * ROW0 + 8 + b, size, stride=2)
                            value = (f0[c, at, :], f0[4 + c, at, :])
                        else:
                            at = pl.ds((2 * i + a) * 8 + b, size, stride=2)
                            value = ((p1, p2)[level - 1][c, at, :], (p1, p2)[level - 1][4 + c, at, :])
                        row = slice(2 * a + b, 2 * a + b + 1)
                        t_re, t_im = shf[level, row, lanes(c)], shf[level, row, lanes(4 + c)]
                        re = t_re * value[0] - t_im * value[1]
                        im = t_re * value[1] + t_im * value[0]
                        acc = (re, im) if acc is None else (acc[0] + re, acc[1] + im)
                dest[c, i * 8 : i * 8 + size, :] = acc[0].astype(BF16).astype(F32)
                dest[4 + c, i * 8 : i * 8 + size, :] = acc[1].astype(BF16).astype(F32)

    def put(c, at, lo, hi):
        me[c, at, :] = jnp.where(even, hi, lo)
        mo[c, at, :] = jnp.where(even, lo, hi)

    for r in range(2):
        for c in range(4):
            lo = c0[c, pl.ds(r, 16, stride=16), :]
            hi = c0[c, pl.ds(14 + r, 16, stride=16), :]
            for h in range(2):
                put(c + 4 * h, pl.ds(r, 8, stride=2), lo[8 * h : 8 * h + 8], hi[8 * h : 8 * h + 8])
        for c in range(8):
            put(c, pl.ds(16 + r, 8, stride=2), p1[c, pl.ds(r, 8, stride=8), :], p1[c, pl.ds(6 + r, 8, stride=8), :])
            put(c, pl.ds(32 + r, 4, stride=2), p2[c, pl.ds(r, 4, stride=8), :], p2[c, pl.ds(2 + r, 4, stride=8), :])
            both = p3[c, pl.ds(r, 2, stride=8), :]
            put(c, pl.ds(40 + r, 2, stride=2), both, both)
    for c in range(8):
        me[c, 44:48, :] = jnp.zeros((4, 128), F32)
        mo[c, 44:48, :] = jnp.zeros((4, 128), F32)
        m_even[c] = me[c].astype(BF16)
        m_odd[c] = mo[c].astype(BF16)


def leaf(f0, ts, inc, i):
    for c in range(4):
        acc = {}
        for xs in range(6):
            if not 0 <= 2 * i + xs - 2 < N0:
                continue
            for k in range(6):
                if xs in (2, 3) and k in (2, 3):
                    continue
                value = values(f0, c, pl.ds((2 * i + xs) * ROW0 + 6 + k, 8, stride=2))
                for a in range(2):
                    for b in range(2):
                        dx, dy = xs - 2 - a, k - 2 - b
                        if far(dx, dy):
                            acc[a, b] = add_product(acc.get((a, b)), factors(ts, 0, dx, dy, c), value)
        for (a, b), sums in acc.items():
            for q, total in enumerate(complex_sum(sums)):
                inc[4 * q + c, pl.ds((2 * i + a) * 16 + b, 8, stride=2), :] = total


def inside(f0, tr, inc, ts):
    re, im = tr[:, :, 0:512], tr[:, :, 512:1024]
    ts[:, :, 0:512] = re
    ts[:, :, 512:1024] = im - re
    ts[:, :, 1024:1536] = re + im
    for i in range(FIRST):
        leaf(f0, ts, inc, i)


def received(axis, r_even, r_odd, lo, hi):
    me = lax.axis_index(axis)
    last = lax.axis_size(axis) - 1
    even = (me % 2) == 0
    for c in range(8):
        from_even = r_even[c].astype(F32)
        from_odd = r_odd[c].astype(F32)
        lo[c] = jnp.where(me == 0, 0.0, jnp.where(even, from_odd, from_even))
        hi[c] = jnp.where(me == last, 0.0, jnp.where(even, from_even, from_odd))


def strips(r_even, r_odd, msk, p1, p2, p3, x_even, x_odd, ylo, yhi, mlo, mhi):
    received("col", r_even, r_odd, ylo, yhi)
    even = (lax.axis_index("row") % 2) == 0
    for dest, first in ((mlo, 0), (mhi, 1)):
        for xr in range(2):
            x = 14 * first + xr
            kept = msk[x].astype(F32)
            for c in range(4):
                dest[4 * xr + c, 2:18, :] = kept[:, lanes(c)]
                at = slice(2 * (x % 8), 2 * (x % 8) + 2)
                dest[4 * xr + c, 0:2, :] = ylo[c + 4 * (x // 8), at, :]
                dest[4 * xr + c, 18:20, :] = yhi[c + 4 * (x // 8), at, :]
            for c in range(8):
                for level_ref, size, base, within in ((p1, 8, 32, 16), (p2, 4, 56, 32), (p3, 2, 20, 40)):
                    x = (size - 2) * first + xr
                    at = base + (size + 4) * xr
                    dest[c, at + 2 : at + 2 + size, :] = level_ref[c, x * 8 : x * 8 + size, :]
                    dest[c, at : at + 2, :] = ylo[c, within + 2 * x : within + 2 * x + 2, :]
                    dest[c, at + 2 + size : at + 4 + size, :] = yhi[c, within + 2 * x : within + 2 * x + 2, :]
    for c in range(8):
        lo = mlo[c]
        hi = mhi[c]
        x_even[c] = jnp.where(even, hi, lo).astype(BF16)
        x_odd[c] = jnp.where(even, lo, hi).astype(BF16)


def beside_y(
    r_even, r_odd, msk, f0, p1, p2, p3, inc0, rad, near, tr, ts, base0, near_base, t_rr, t_ii, own1, own2, own3,
    ylo, yhi, hy, hc, f1, g1, box, swapped, out, cx, ln,
):
    received("col", r_even, r_odd, ylo, yhi)
    blocks = []
    zero = jnp.zeros((8, 128), F32)
    for s, src in enumerate((ylo, yhi)):
        for r in range(2):
            both = [
                jnp.concatenate([src[4 * h + c, pl.ds(r, 8, stride=2), :] for c in range(4)], axis=1) for h in range(2)
            ]
            blocks.append(jnp.concatenate(both, axis=0))
        touching = blocks[2 * s + 1 - s]
        for c in range(4):
            hc[s, c, 0:8, :] = zero
            hc[s, c, 8:24, :] = touching[:, lanes(c)]
            hc[s, c, 24:32, :] = zero
    halo = jnp.dot(jnp.concatenate(blocks, axis=0).astype(BF16), rad[...], preferred_element_type=F32)
    halo = halo.astype(BF16).astype(F32)
    for c in range(4):
        re, im = halo[:, lanes(c)], halo[:, lanes(4 + c)]
        for q, part in enumerate((re, im, re + im)):
            for n in range(4):
                hy[4 * q + c, n * 32 : n * 32 + 8, :] = zero
                hy[4 * q + c, n * 32 + 8 : n * 32 + 24, :] = part[16 * n : 16 * n + 16]
                hy[4 * q + c, n * 32 + 24 : n * 32 + 32, :] = zero
    for dx in range(-3, 4):
        for dy in range(-3, 4):
            if far(dx, dy):
                row = (dx + 3) * 7 + dy + 3
                for c in range(4):
                    re = tr[row, 2:4, lanes(c)]
                    im = tr[row, 2:4, lanes(4 + c)]
                    t_rr[pl.ds(row * 8 + c, 2, stride=392), :] = re
                    t_rr[pl.ds(row * 8 + 4 + c, 2, stride=392), :] = re
                    t_ii[pl.ds(row * 8 + c, 2, stride=392), :] = -im
                    t_ii[pl.ds(row * 8 + 4 + c, 2, stride=392), :] = im
    for c in range(8):
        base0[c, 0 : FIRST * 32, :] = inc0[c]
    for i in range(FIRST, 8):
        leaf(f0, ts, base0, i)
    for x in range(N0):
        kept = msk[x].astype(F32)
        for c in range(4):
            cx[c, x * ROW0 : x * ROW0 + 8, :] = zero
            cx[c, x * ROW0 + 8 : x * ROW0 + 24, :] = kept[:, lanes(c)]
            cx[c, x * ROW0 + 24 : x * ROW0 + 32, :] = zero
    ln[0] = jnp.zeros((16, 1536), BF16)
    ln[17] = jnp.zeros((16, 1536), BF16)
    for dy in range(3):
        for x in range(N0):
            for c in range(4):
                at = x * ROW0 + 7 + dy
                ln[x + 1, :, lanes(4 * dy + c)] = cx[c, at : at + 16, :].astype(BF16)
    total = None
    for dx in range(3):
        rows = ln[dx : dx + 16].reshape(N0 * N0, 1536)
        term = jnp.dot(rows, near[3 * dx : 3 * dx + 3].reshape(1536, 512), preferred_element_type=F32)
        total = term if total is None else total + term
    for c in range(4):
        near_base[c] = total[:, lanes(c)]
    for s in range(2):
        for c in range(4):
            acc = {}
            for r in range(2):
                for xs in range(6):
                    value = values(hy, c, pl.ds((2 * s + r) * 32 + 6 + xs, 8, stride=2))
                    for a in range(2):
                        for b in range(2):
                            dx, dy = xs - 2 - a, 4 * s - 2 + r - b
                            if far(dx, dy):
                                acc[a, b] = add_product(acc.get((a, b)), factors(ts, 0, dx, dy, c), value)
            for (a, b), sums in acc.items():
                for q, total in enumerate(complex_sum(sums)):
                    at = pl.ds(16 * a + 14 * s + b, 8, stride=32)
                    base0[4 * q + c, at, :] = base0[4 * q + c, at, :] + total
        total = None
        for dx in range(3):
            rows = jnp.concatenate([hc[s, c, 7 + dx : 23 + dx, :] for c in range(4)], axis=1).astype(BF16)
            term = jnp.dot(rows, near[3 * dx + 2 * s], preferred_element_type=F32)
            total = term if total is None else total + term
        for c in range(4):
            at = pl.ds(15 * s, 16, stride=16)
            near_base[c, at, :] = near_base[c, at, :] + total[:, lanes(c)]
    for level, size, own, base, inc in ((3, 2, p3, 40, own3), (2, 4, p2, 32, own2)):
        rows = [
            (x + 2, [(2, size, own, x * 8), (0, 2, ylo, base + 2 * x), (size + 2, 2, yhi, base + 2 * x)])
            for x in range(size)
        ]
        by_box(level, size, rows, t_rr, t_ii, box, swapped, out)
        for c in range(8):
            for x in range(size):
                inc[c, x * 8 : x * 8 + size, :] = out[pl.ds(x * size * 8 + c, size, stride=8), :]
    for c in range(8):
        for x in range(8):
            base = x * ROWS
            f1[c, base + 8 : base + 16, :] = p1[c, x * 8 : x * 8 + 8, :]
            f1[c, base + 6 : base + 8, :] = ylo[c, 16 + 2 * x : 18 + 2 * x, :]
            f1[c, base + 16 : base + 18, :] = yhi[c, 16 + 2 * x : 18 + 2 * x, :]
    for c in range(4):
        for s in range(3):
            for xe in range(8):
                for h in range(2):
                    x = xe + 4 * h - 2
                    at = slice(xe * 16 + 8 * h, xe * 16 + 8 * h + 8)
                    if 0 <= x < 8:
                        base = x * ROWS + 6 + 2 * s
                        re, im = f1[c, base : base + 8, :], f1[4 + c, base : base + 8, :]
                        parts = (re, im, re + im)
                    else:
                        parts = (zero, zero, zero)
                    for q, part in enumerate(parts):
                        g1[s, 4 * q + c, at, :] = part
    for i in range(2):
        for c in range(4):
            acc = {}
            for xs in range(6):
                for k in range(6):
                    if xs in (2, 3) and k in (2, 3):
                        continue
                    at = pl.ds((2 * i + xs) * 16 + k % 2, 8, stride=2)
                    value = [g1[k // 2, 4 * q + c, at, :] for q in range(3)]
                    for a in range(2):
                        for b in range(2):
                            dx, dy = xs - 2 - a, k - 2 - b
                            if far(dx, dy):
                                acc[a, b] = add_product(acc.get((a, b)), factors(ts, 1, dx, dy, c), value)
            for (a, b), sums in acc.items():
                for q, total in enumerate(complex_sum(sums)):
                    for h in range(2):
                        at = pl.ds((2 * (i + 2 * h) + a) * 8 + b, 4, stride=2)
                        own1[4 * q + c, at, :] = total[4 * h : 4 * h + 4]


def add_parent(inc, parent, shf, level, size):
    half = size // 2
    for x in range(size):
        for b in range(2):
            row = slice(2 * (x % 2) + b, 2 * (x % 2) + b + 1)
            at = pl.ds(x * 8 + b, half, stride=2)
            for c in range(4):
                q_re = parent[c, (x // 2) * 8 : (x // 2) * 8 + half, :]
                q_im = parent[4 + c, (x // 2) * 8 : (x // 2) * 8 + half, :]
                t_re = shf[level, row, lanes(c)]
                t_im = shf[level, row, lanes(4 + c)]
                inc[c, at, :] = inc[c, at, :] + (t_re * q_re + t_im * q_im)
                inc[4 + c, at, :] = inc[4 + c, at, :] + (t_re * q_im - t_im * q_re)


def by_box(level, size, rows, t_rr, t_ii, box, swapped, out):
    wide = size + 4
    for c in range(8):
        for xe, pieces in rows:
            for ye, count, src, at in pieces:
                piece = src[c, at : at + count, :]
                first = (xe * wide + ye) * 8
                box[pl.ds(first + c, count, stride=8), :] = piece
                swapped[pl.ds(first + (c + 4) % 8, count, stride=8), :] = piece
    given = [xe for xe, _ in rows]
    for i in range(size // 2):
        for j in range(size // 2):
            acc = {}
            for xs in range(6):
                if 2 * i + xs not in given:
                    continue
                for k in range(6):
                    if xs in (2, 3) and k in (2, 3):
                        continue
                    at = ((2 * i + xs) * wide + 2 * j + k) * 8
                    value = box[at : at + 8, :]
                    other = swapped[at : at + 8, :]
                    for a in range(2):
                        for b in range(2):
                            dx, dy = xs - 2 - a, k - 2 - b
                            if far(dx, dy):
                                row = (level - 2) * 392 + ((dx + 3) * 7 + dy + 3) * 8
                                term = t_rr[row : row + 8, :] * value + t_ii[row : row + 8, :] * other
                                acc[a, b] = term if (a, b) not in acc else acc[a, b] + term
            for a in range(2):
                for b in range(2):
                    at = ((2 * i + a) * size + 2 * j + b) * 8
                    out[at : at + 8, :] = acc.get((a, b), jnp.zeros((8, 128), F32))


def downward(
    cnt, inc0, near_base, t_rr, t_ii, own1, own2, own3, x_even, x_odd, rad, rec, near, ts, shf,
    field, xlo, xhi, hc, hx, xs1, box, swapped, out, tot, inc1, inc2, inc3, half,
):
    received("row", x_even, x_odd, xlo, xhi)
    sides = []
    for s, src in enumerate((xlo, xhi)):
        for xr in range(2):
            sides.append(jnp.concatenate([src[4 * xr + c, 0:32, :] for c in range(4)], axis=1))
        for c in range(4):
            hc[s, c, 0:24, :] = src[4 * (1 - s) + c, 0:24, :]
    halo = jnp.dot(jnp.concatenate(sides, axis=0).astype(BF16), rad[...], preferred_element_type=F32)
    halo = halo.astype(BF16).astype(F32)
    for c in range(4):
        re, im = halo[:, lanes(c)], halo[:, lanes(4 + c)]
        for q, part in enumerate((re, im, re + im)):
            hx[4 * q + c] = part
        for s, src in enumerate((xlo, xhi)):
            re, im = src[c, 32:56, :], src[4 + c, 32:56, :]
            for q, part in enumerate((re, im, re + im)):
                xs1[4 * q + c, s * 24 : s * 24 + 24, :] = part

    for level, size, base, own, inc in ((3, 2, 20, own3, inc3), (2, 4, 56, own2, inc2)):
        wide = size + 4
        rows = [
            (xe + xr, [(0, wide, src, base + wide * xr)]) for src, xe in ((xlo, 0), (xhi, size + 2)) for xr in range(2)
        ]
        by_box(level, size, rows, t_rr, t_ii, box, swapped, out)
        for c in range(8):
            for x in range(size):
                at = slice(x * 8, x * 8 + size)
                inc[c, at, :] = own[c, at, :] + out[pl.ds(x * size * 8 + c, size, stride=8), :]
    add_parent(inc2, inc3, shf, 2, 4)
    for c in range(8):
        inc1[c] = own1[c]
    for s in range(2):
        for c in range(4):
            acc = {}
            for xr in range(2):
                xs = 4 * s + xr
                for k in range(6):
                    value = values(xs1, c, pl.ds((2 * s + xr) * 12 + k, 4, stride=2))
                    for a in range(2):
                        for b in range(2):
                            dx, dy = xs - 2 - a, k - 2 - b
                            if far(dx, dy):
                                acc[a, b] = add_product(acc.get((a, b)), factors(ts, 1, dx, dy, c), value)
            for (a, b), sums in acc.items():
                at = pl.ds((6 * s + a) * 8 + b, 4, stride=2)
                for q, total in enumerate(complex_sum(sums)):
                    inc1[4 * q + c, at, :] = inc1[4 * q + c, at, :] + total
    add_parent(inc1, inc2, shf, 1, 8)

    for x in range(N0):
        for b in range(2):
            row = slice(2 * (x % 2) + b, 2 * (x % 2) + b + 1)
            at = pl.ds(x * 16 + b, 8, stride=2)
            for c in range(4):
                q_re = inc1[c, (x // 2) * 8 : (x // 2) * 8 + 8, :]
                q_im = inc1[4 + c, (x // 2) * 8 : (x // 2) * 8 + 8, :]
                t_re = shf[0, row, lanes(c)]
                t_im = shf[0, row, lanes(4 + c)]
                tot[c, at, :] = inc0[c, at, :] + (t_re * q_re + t_im * q_im)
                tot[4 + c, at, :] = inc0[4 + c, at, :] + (t_re * q_im - t_im * q_re)
    for s in range(2):
        for c in range(4):
            acc = {}
            for xr in range(2):
                xs = 4 * s + xr
                for k in range(6):
                    value = values(hx, c, pl.ds((2 * s + xr) * 32 + k, 8, stride=2))
                    for a in range(2):
                        for b in range(2):
                            dx, dy = xs - 2 - a, k - 2 - b
                            if far(dx, dy):
                                acc[a, b] = add_product(acc.get((a, b)), factors(ts, 0, dx, dy, c), value)
            for (a, b), sums in acc.items():
                at = pl.ds((14 * s + a) * 16 + b, 8, stride=2)
                for q, total in enumerate(complex_sum(sums)):
                    tot[4 * q + c, at, :] = tot[4 * q + c, at, :] + total
    for c in range(8):
        half[:, lanes(c)] = tot[c].astype(BF16)
    side = []
    for s in range(2):
        total = None
        for dy in range(3):
            rows = jnp.concatenate([hc[s, c, 1 + dy : 17 + dy, :] for c in range(4)], axis=1).astype(BF16)
            term = jnp.dot(rows, near[6 * s + dy], preferred_element_type=F32)
            total = term if total is None else total + term
        side.append(total)
    total = jnp.dot(half[...], rec[...], preferred_element_type=F32)
    for x in range(N0):
        here = slice(x * 16, (x + 1) * 16)
        result = total[here] + jnp.concatenate([near_base[c, here, :] for c in range(4)], axis=1)
        if x in (0, N0 - 1):
            result = result + side[x // (N0 - 1)]
        field[x] = jnp.where(occupied_rows(cnt, x), result, 0.0).astype(BF16)


def call(kernel, outs, scratch, flops, *args):
    place = pl.BlockSpec(memory_space=pltpu.VMEM)
    return pl.pallas_call(
        kernel,
        out_shape=outs,
        in_specs=[place] * len(args),
        out_specs=[place] * len(outs),
        scratch_shapes=scratch,
        compiler_params=pltpu.CompilerParams(vmem_limit_bytes=16 * 1024 * 1024),
        cost_estimate=pl.CostEstimate(flops=flops, bytes_accessed=1 << 20, transcendentals=0),
        interpret=INTERPRET,
    )(*args)


def shape(dims, kind):
    return jax.ShapeDtypeStruct(dims, kind)


def swap(value, axis, odd):
    return lax.ppermute(value, ("row", "col"), swap_perm(axis, odd))


def shards(currents, counts, radiate, receive, near_blocks, translate, shift):
    mem = pltpu.VMEM
    factor = jnp.transpose(translate, (1, 0, 2))
    ys, xs = mem((8, SY, 128), F32), mem((8, SX, 128), F32)
    (first,) = call(opening, [shape((8, 128), F32)], [], 10**13)
    masked, f0, p1, p2, p3, m_even, m_odd = call(
        upward,
        [
            shape((16, 16, 512), BF16),
            shape((12, 20 * ROW0, 128), F32),
            shape((8, 64, 128), F32),
            shape((8, 32, 128), F32),
            shape((8, 16, 128), F32),
            shape((8, SY, 128), BF16),
            shape((8, SY, 128), BF16),
        ],
        [mem((4, 256, 128), F32), ys, ys],
        10**12,
        first, currents, counts, radiate, shift,
    )
    r_even = swap(m_even, "col", 0)
    r_odd = swap(m_odd, "col", 1)
    inc0, sums = call(
        inside,
        [shape((8, 32 * FIRST, 128), F32), shape((49, 4, 1536), F32)],
        [],
        4 * 10**9,
        f0, factor,
    )
    r_even, r_odd, inc0 = lax.optimization_barrier((r_even, r_odd, inc0))
    s_even, s_odd = call(
        strips,
        [shape((8, SX, 128), BF16)] * 2,
        [ys, ys, xs, xs],
        10**7,
        r_even, r_odd, masked, p1, p2, p3,
    )
    x_even = swap(s_even, "row", 0)
    x_odd = swap(s_odd, "row", 1)
    inc0, near_sum, t_rr, t_ii, own1, own2, own3 = call(
        beside_y,
        [
            shape((8, 256, 128), F32), shape((4, 256, 128), F32), shape((784, 128), F32), shape((784, 128), F32),
            shape((8, 64, 128), F32), shape((8, 32, 128), F32), shape((8, 16, 128), F32),
        ],
        [
            ys, ys, mem((12, 128, 128), F32), mem((2, 4, 32, 128), F32), mem((8, 8 * ROWS, 128), F32),
            mem((3, 12, 128, 128), F32), mem((512, 128), F32), mem((512, 128), F32), mem((128, 128), F32),
            mem((4, 16 * ROW0, 128), F32), mem((18, 16, 1536), BF16),
        ],
        10**9,
        r_even, r_odd, masked, f0, p1, p2, p3, inc0, radiate, near_blocks, factor, sums,
    )
    (field,) = call(
        downward,
        [shape((16, 16, 512), BF16)],
        [
            xs, xs, mem((2, 4, 24, 128), F32), mem((12, 128, 128), F32), mem((12, 48, 128), F32),
            mem((512, 128), F32), mem((512, 128), F32), mem((128, 128), F32),
            mem((8, 256, 128), F32), mem((8, 64, 128), F32), mem((8, 32, 128), F32), mem((8, 16, 128), F32),
            mem((256, 1024), BF16),
        ],
        3 * 10**9,
        counts, inc0, near_sum, t_rr, t_ii, own1, own2, own3, x_even, x_odd,
        radiate, receive, near_blocks, sums, shift,
    )
    return field


def solution(mesh):
    return jax.shard_map(
        shards,
        mesh=mesh,
        in_specs=(P("row", "col", None), P("row", "col"), P(), P(), P(), P(), P()),
        out_specs=P("row", "col", None),
        check_vma=False,
    )
```

```python
import jax
import jax.numpy as jnp
from jax import lax
from jax.experimental import pallas as pl
from jax.experimental.pallas import tpu as pltpu
from jax.sharding import PartitionSpec as P

U = 16
INTERPRET = False
F32 = jnp.float32
BF16 = jnp.bfloat16
N0 = 16
ROW0 = 32
ROWS = 24
SX = 72
MX = 48
SY = 48
FIRST = 7


def far(dx, dy):
    return max(abs(dx), abs(dy)) >= 2 and max(abs(dx), abs(dy)) <= 3


def lanes(c):
    return slice(c * 128, (c + 1) * 128)


def factors(ts, level, dx, dy, c):
    row = (dx + 3) * 7 + dy + 3
    return [ts[row, level : level + 1, lanes(4 * n + c)] for n in range(3)]


def values(ref, c, at):
    return [ref[4 * n + c, at, :] for n in range(3)]


def count_rows(cnt_ref, x):
    row = cnt_ref[x : x + 1, :].astype(F32)
    one = lax.broadcasted_iota(jnp.int32, (N0, N0), 0) == lax.broadcasted_iota(jnp.int32, (N0, N0), 1)
    return jnp.sum(jnp.where(one, jnp.broadcast_to(row, (N0, N0)), 0.0), axis=1, keepdims=True)


def occupied(count, c):
    lane = lax.broadcasted_iota(jnp.int32, count.shape, 1).astype(F32) + float(128 * c)
    return lane < count * float(2 * U)


def swap_perm(axis, odd):
    size = (lax.axis_size("row"), lax.axis_size("col"))
    which = ("row", "col").index(axis)
    perm = []
    for row in range(size[0]):
        for col in range(size[1]):
            at = [row, col]
            to = at[which] + (1 if at[which] % 2 == odd else -1)
            if 0 <= to < size[which]:
                at[which] = to
            else:
                at[1 - which] ^= 1
            perm.append((row * size[1] + col, at[0] * size[1] + at[1]))
    return perm


def add_product(acc, factor, value):
    terms = (factor[0] * value[2], factor[1] * value[0], factor[2] * value[1])
    return terms if acc is None else tuple(old + term for old, term in zip(acc, terms))


def complex_sum(acc):
    return acc[0] - acc[2], acc[0] + acc[1]


def opening(f0):
    zero = jnp.zeros((8, 128), F32)
    for c in range(12):
        for x in range(N0):
            base = (x + 2) * ROW0
            f0[c, base : base + 8, :] = zero
            f0[c, base + 24 : base + 32, :] = zero


def mask(cur, cnt, msk, c0, count):
    for x in range(N0):
        here = slice(x * 16, (x + 1) * 16)
        count[here, :] = jnp.broadcast_to(count_rows(cnt, x), (N0, 128))
        for c in range(4):
            kept = jnp.where(occupied(count[here, :], c), cur[x, :, lanes(c)].astype(F32), 0.0)
            msk[x, :, lanes(c)] = kept.astype(BF16)
            c0[c, here, :] = kept


def upward(f0_zero, msk, c0, rad, shf, f0, p1, p2, p3, m_odd, m_even, me, mo):
    even = (lax.axis_index("col") % 2) == 0
    lhs = msk[...].reshape(N0 * N0, 512)
    for m in range(2):
        re, im = [
            jnp.dot(lhs, rad[:, n : n + 256], preferred_element_type=F32).astype(BF16).astype(F32)
            for n in (256 * m, 512 + 256 * m)
        ]
        for n, out in enumerate((re, im, re + im)):
            for h in range(2):
                for x in range(N0):
                    base = (x + 2) * ROW0
                    c = 4 * n + 2 * m + h
                    f0[c, base + 8 : base + 24, :] = out[x * 16 : (x + 1) * 16, lanes(h)]
    for level, (dest, size) in enumerate(((p1, 8), (p2, 4), (p3, 2))):
        for i in range(size):
            for c in range(4):
                acc = None
                for a in range(2):
                    for b in range(2):
                        if level == 0:
                            at = pl.ds((2 * i + a + 2) * ROW0 + 8 + b, size, stride=2)
                            value = (f0[c, at, :], f0[4 + c, at, :])
                        else:
                            at = pl.ds((2 * i + a) * 8 + b, size, stride=2)
                            value = ((p1, p2)[level - 1][c, at, :], (p1, p2)[level - 1][4 + c, at, :])
                        row = slice(2 * a + b, 2 * a + b + 1)
                        t_re, t_im = shf[level, row, lanes(c)], shf[level, row, lanes(4 + c)]
                        re = t_re * value[0] - t_im * value[1]
                        im = t_re * value[1] + t_im * value[0]
                        acc = (re, im) if acc is None else (acc[0] + re, acc[1] + im)
                dest[c, i * 8 : i * 8 + size, :] = acc[0].astype(BF16).astype(F32)
                dest[4 + c, i * 8 : i * 8 + size, :] = acc[1].astype(BF16).astype(F32)

    def put(c, at, lo, hi):
        me[c, at, :] = jnp.where(even, hi, lo)
        mo[c, at, :] = jnp.where(even, lo, hi)

    for r in range(2):
        for c in range(4):
            lo = c0[c, pl.ds(r, 16, stride=16), :]
            hi = c0[c, pl.ds(14 + r, 16, stride=16), :]
            for h in range(2):
                put(c + 4 * h, pl.ds(r, 8, stride=2), lo[8 * h : 8 * h + 8], hi[8 * h : 8 * h + 8])
        for c in range(8):
            put(c, pl.ds(16 + r, 8, stride=2), p1[c, pl.ds(r, 8, stride=8), :], p1[c, pl.ds(6 + r, 8, stride=8), :])
            put(c, pl.ds(32 + r, 4, stride=2), p2[c, pl.ds(r, 4, stride=8), :], p2[c, pl.ds(2 + r, 4, stride=8), :])
            both = p3[c, pl.ds(r, 2, stride=8), :]
            put(c, pl.ds(40 + r, 2, stride=2), both, both)
    for c in range(8):
        me[c, 44:48, :] = jnp.zeros((4, 128), F32)
        mo[c, 44:48, :] = jnp.zeros((4, 128), F32)
        m_even[c] = me[c].astype(BF16)
        m_odd[c] = mo[c].astype(BF16)


def leaf(f0, ts, inc, i):
    for c in range(4):
        acc = {}
        for xs in range(6):
            if not 0 <= 2 * i + xs - 2 < N0:
                continue
            for k in range(6):
                if xs in (2, 3) and k in (2, 3):
                    continue
                value = values(f0, c, pl.ds((2 * i + xs) * ROW0 + 6 + k, 8, stride=2))
                for a in range(2):
                    for b in range(2):
                        dx, dy = xs - 2 - a, k - 2 - b
                        if far(dx, dy):
                            acc[a, b] = add_product(acc.get((a, b)), factors(ts, 0, dx, dy, c), value)
        for (a, b), sums in acc.items():
            for q, total in enumerate(complex_sum(sums)):
                inc[4 * q + c, pl.ds((2 * i + a) * 16 + b, 8, stride=2), :] = total


def inside(f0, tr, inc, ts, t_rr, t_ii):
    re, im = tr[:, :, 0:512], tr[:, :, 512:1024]
    ts[:, :, 0:512] = re
    ts[:, :, 512:1024] = im - re
    ts[:, :, 1024:1536] = re + im
    offsets = [(dx, dy) for dx in range(-3, 4) for dy in range(-3, 4) if far(dx, dy)]
    for i in range(FIRST):
        leaf(f0, ts, inc, i)
        for dx, dy in offsets[i::FIRST]:
            row = (dx + 3) * 7 + dy + 3
            for c in range(4):
                re = tr[row, 2:4, lanes(c)]
                im = tr[row, 2:4, lanes(4 + c)]
                t_rr[pl.ds(row * 8 + c, 2, stride=392), :] = re
                t_rr[pl.ds(row * 8 + 4 + c, 2, stride=392), :] = re
                t_ii[pl.ds(row * 8 + c, 2, stride=392), :] = -im
                t_ii[pl.ds(row * 8 + 4 + c, 2, stride=392), :] = im


def received(axis, r_even, r_odd, lo, hi):
    me = lax.axis_index(axis)
    last = lax.axis_size(axis) - 1
    even = (me % 2) == 0
    for c in range(8):
        from_even = r_even[c].astype(F32)
        from_odd = r_odd[c].astype(F32)
        lo[c] = jnp.where(me == 0, 0.0, jnp.where(even, from_odd, from_even))
        hi[c] = jnp.where(me == last, 0.0, jnp.where(even, from_even, from_odd))


def strips(
    r_odd, r_even, msk, p1, p2, p3, ts, t_rr, t_ii, x_even, x_odd,
    ylo, yhi, mlo, mhi, xs1, left, right, box2, swp2, out2, box3, swp3, out3, box4, swp4, out4,
):
    received("col", r_even, r_odd, ylo, yhi)
    even = (lax.axis_index("row") % 2) == 0
    for dest, first in ((mlo, 0), (mhi, 1)):
        for xr in range(2):
            x = 14 * first + xr
            kept = msk[x].astype(F32)
            for c in range(4):
                dest[4 * xr + c, 2:18, :] = kept[:, lanes(c)]
                at = slice(2 * (x % 8), 2 * (x % 8) + 2)
                dest[4 * xr + c, 0:2, :] = ylo[c + 4 * (x // 8), at, :]
                dest[4 * xr + c, 18:20, :] = yhi[c + 4 * (x // 8), at, :]
            for c in range(8):
                for level_ref, size, base, within in ((p1, 8, 32, 16), (p2, 4, 56, 32), (p3, 2, 20, 40)):
                    x = (size - 2) * first + xr
                    at = base + (size + 4) * xr
                    dest[c, at + 2 : at + 2 + size, :] = level_ref[c, x * 8 : x * 8 + size, :]
                    dest[c, at : at + 2, :] = ylo[c, within + 2 * x : within + 2 * x + 2, :]
                    dest[c, at + 2 + size : at + 4 + size, :] = yhi[c, within + 2 * x : within + 2 * x + 2, :]
    both = ((right, mhi), (left, mlo))
    for c in range(4):
        for s, (_, src) in enumerate(both):
            re, im = src[c, 32:56, :], src[4 + c, 32:56, :]
            for q, part in enumerate((re, im, re + im)):
                xs1[4 * q + c, s * 24 : s * 24 + 24, :] = part
    for s, (message, src) in enumerate(both):
        for c in range(8):
            message[c, 0:20, :] = src[c, 0:20, :]
        for c in range(4):
            acc = {}
            for xr in range(2):
                xs = 4 * s + xr
                for k in range(6):
                    value = values(xs1, c, pl.ds((2 * s + xr) * 12 + k, 4, stride=2))
                    for a in range(2):
                        for b in range(2):
                            dx, dy = xs - 2 - a, k - 2 - b
                            if far(dx, dy):
                                acc[a, b] = add_product(acc.get((a, b)), factors(ts, 1, dx, dy, c), value)
            for (a, b), sums in acc.items():
                for q, total in enumerate(complex_sum(sums)):
                    message[4 * q + c, pl.ds(32 + 8 * a + b, 4, stride=2), :] = total
    rows = [(6 * s + xr, [(0, 8, src, 56 + 8 * xr)]) for s, (_, src) in enumerate(both) for xr in range(2)]
    by_box(2, 4, rows, t_rr, t_ii, box2, swp2, out2)
    for s, (message, src) in enumerate(both):
        box, swapped, out = ((box3, swp3, out3), (box4, swp4, out4))[s]
        by_box(3, 2, [(4 * s + xr, [(0, 6, src, 20 + 6 * xr)]) for xr in range(2)], t_rr, t_ii, box, swapped, out)
        for c in range(8):
            message[c, 20:24, :] = out[pl.ds(c, 4, stride=8), :]
            for a in range(2):
                message[c, 24 + 4 * a : 28 + 4 * a, :] = out2[pl.ds((2 * s + a) * 32 + c, 4, stride=8), :]
    for c in range(8):
        lo = left[c]
        hi = right[c]
        x_even[c] = jnp.where(even, hi, lo).astype(BF16)
        x_odd[c] = jnp.where(even, lo, hi).astype(BF16)


def beside_y(
    r_odd, r_even, msk, f0, p1, p2, p3, inc0, rad, near, ts, t_rr, t_ii, base0, near_base, own1, own2, own3,
    ylo, yhi, hy, f1, g1, box2, swp2, out2, box3, swp3, out3, cx, ln,
):
    received("col", r_even, r_odd, ylo, yhi)
    blocks = []
    zero = jnp.zeros((8, 128), F32)
    for x in range(N0):
        kept = msk[x].astype(F32)
        for c in range(4):
            cx[c, x * ROW0 + 8 : x * ROW0 + 24, :] = kept[:, lanes(c)]
    for s, src in enumerate((ylo, yhi)):
        for r in range(2):
            both = [
                jnp.concatenate([src[4 * h + c, pl.ds(r, 8, stride=2), :] for c in range(4)], axis=1) for h in range(2)
            ]
            blocks.append(jnp.concatenate(both, axis=0))
        touching = blocks[2 * s + 1 - s]
        for c in range(4):
            cx[c, pl.ds(7 + 17 * s, 16, stride=ROW0), :] = touching[:, lanes(c)]
    halo = jnp.dot(jnp.concatenate(blocks, axis=0).astype(BF16), rad[...], preferred_element_type=F32)
    halo = halo.astype(BF16).astype(F32)
    for c in range(4):
        re, im = halo[:, lanes(c)], halo[:, lanes(4 + c)]
        for q, part in enumerate((re, im, re + im)):
            for n in range(4):
                hy[4 * q + c, n * 32 : n * 32 + 8, :] = zero
                hy[4 * q + c, n * 32 + 8 : n * 32 + 24, :] = part[16 * n : 16 * n + 16]
                hy[4 * q + c, n * 32 + 24 : n * 32 + 32, :] = zero
    ln[0] = jnp.zeros((16, 1536), BF16)
    ln[17] = jnp.zeros((16, 1536), BF16)
    for dy in range(3):
        for x in range(N0):
            for c in range(4):
                at = x * ROW0 + 7 + dy
                ln[x + 1, :, lanes(4 * dy + c)] = cx[c, at : at + 16, :].astype(BF16)
    for c in range(8):
        for x in range(8):
            base = x * ROWS
            f1[c, base + 8 : base + 16, :] = p1[c, x * 8 : x * 8 + 8, :]
            f1[c, base + 6 : base + 8, :] = ylo[c, 16 + 2 * x : 18 + 2 * x, :]
            f1[c, base + 16 : base + 18, :] = yhi[c, 16 + 2 * x : 18 + 2 * x, :]
    for c in range(4):
        for s in range(3):
            for xe in range(8):
                for h in range(2):
                    x = xe + 4 * h - 2
                    at = slice(xe * 16 + 8 * h, xe * 16 + 8 * h + 8)
                    if 0 <= x < 8:
                        base = x * ROWS + 6 + 2 * s
                        re, im = f1[c, base : base + 8, :], f1[4 + c, base : base + 8, :]
                        parts = (re, im, re + im)
                    else:
                        parts = (zero, zero, zero)
                    for q, part in enumerate(parts):
                        g1[s, 4 * q + c, at, :] = part
    for c in range(8):
        base0[c, 0 : FIRST * 32, :] = inc0[c]

    def near_term(n):
        dx, h = n % 3, n // 3
        rows = ln[dx : dx + 16].reshape(N0 * N0, 1536)
        weights = near[3 * dx : 3 * dx + 3, :, h * 256 : h * 256 + 256].reshape(1536, 256)
        term = jnp.dot(rows, weights, preferred_element_type=F32)
        for q in range(2):
            if dx == 0:
                near_base[2 * h + q] = term[:, lanes(q)]
            else:
                near_base[2 * h + q] = near_base[2 * h + q] + term[:, lanes(q)]

    def across_y(s, c):
        acc = {}
        for r in range(2):
            for xs in range(6):
                value = values(hy, c, pl.ds((2 * s + r) * 32 + 6 + xs, 8, stride=2))
                for a in range(2):
                    for b in range(2):
                        dx, dy = xs - 2 - a, 4 * s - 2 + r - b
                        if far(dx, dy):
                            acc[a, b] = add_product(acc.get((a, b)), factors(ts, 0, dx, dy, c), value)
        for (a, b), sums in acc.items():
            for q, total in enumerate(complex_sum(sums)):
                at = pl.ds(16 * a + 14 * s + b, 8, stride=32)
                base0[4 * q + c, at, :] = base0[4 * q + c, at, :] + total

    def middle(i, c):
        acc = {}
        for xs in range(6):
            for k in range(6):
                if xs in (2, 3) and k in (2, 3):
                    continue
                at = pl.ds((2 * i + xs) * 16 + k % 2, 8, stride=2)
                value = [g1[k // 2, 4 * q + c, at, :] for q in range(3)]
                for a in range(2):
                    for b in range(2):
                        dx, dy = xs - 2 - a, k - 2 - b
                        if far(dx, dy):
                            acc[a, b] = add_product(acc.get((a, b)), factors(ts, 1, dx, dy, c), value)
        for (a, b), sums in acc.items():
            for q, total in enumerate(complex_sum(sums)):
                for h in range(2):
                    at = pl.ds((2 * (i + 2 * h) + a) * 8 + b, 4, stride=2)
                    own1[4 * q + c, at, :] = total[4 * h : 4 * h + 4]

    def small(level):
        size, own, base, inc = {2: (4, p2, 32, own2), 3: (2, p3, 40, own3)}[level]
        box, swapped, out = {2: (box2, swp2, out2), 3: (box3, swp3, out3)}[level]
        rows = [
            (x + 2, [(2, size, own, x * 8), (0, 2, ylo, base + 2 * x), (size + 2, 2, yhi, base + 2 * x)])
            for x in range(size)
        ]
        by_box(level, size, rows, t_rr, t_ii, box, swapped, out)
        for c in range(8):
            for x in range(size):
                inc[c, x * 8 : x * 8 + size, :] = out[pl.ds(x * size * 8 + c, size, stride=8), :]

    for n in range(6):
        near_term(n)
        if n < 4:
            for i in range(2):
                middle(i, n)
        else:
            for c in range(4):
                across_y(n - 4, c)
        if n in (1, 2):
            small(n + 1)
        if n == 3:
            for i in range(FIRST, 8):
                leaf(f0, ts, base0, i)


def add_parent(inc, parent, shf, level, size):
    half = size // 2
    for x in range(size):
        for b in range(2):
            row = slice(2 * (x % 2) + b, 2 * (x % 2) + b + 1)
            at = pl.ds(x * 8 + b, half, stride=2)
            for c in range(4):
                q_re = parent[c, (x // 2) * 8 : (x // 2) * 8 + half, :]
                q_im = parent[4 + c, (x // 2) * 8 : (x // 2) * 8 + half, :]
                t_re = shf[level, row, lanes(c)]
                t_im = shf[level, row, lanes(4 + c)]
                inc[c, at, :] = inc[c, at, :] + (t_re * q_re + t_im * q_im)
                inc[4 + c, at, :] = inc[4 + c, at, :] + (t_re * q_im - t_im * q_re)


def by_box(level, size, rows, t_rr, t_ii, box, swapped, out):
    wide = size + 4
    for c in range(8):
        for xe, pieces in rows:
            for ye, count, src, at in pieces:
                piece = src[c, at : at + count, :]
                first = (xe * wide + ye) * 8
                box[pl.ds(first + c, count, stride=8), :] = piece
                swapped[pl.ds(first + (c + 4) % 8, count, stride=8), :] = piece
    given = [xe for xe, _ in rows]
    for i in range(size // 2):
        for j in range(size // 2):
            acc = {}
            for xs in range(6):
                if 2 * i + xs not in given:
                    continue
                for k in range(6):
                    if xs in (2, 3) and k in (2, 3):
                        continue
                    at = ((2 * i + xs) * wide + 2 * j + k) * 8
                    value = box[at : at + 8, :]
                    other = swapped[at : at + 8, :]
                    for a in range(2):
                        for b in range(2):
                            dx, dy = xs - 2 - a, k - 2 - b
                            if far(dx, dy):
                                row = (level - 2) * 392 + ((dx + 3) * 7 + dy + 3) * 8
                                term = t_rr[row : row + 8, :] * value + t_ii[row : row + 8, :] * other
                                acc[a, b] = term if (a, b) not in acc else acc[a, b] + term
            for a in range(2):
                for b in range(2):
                    at = ((2 * i + a) * size + 2 * j + b) * 8
                    out[at : at + 8, :] = acc.get((a, b), jnp.zeros((8, 128), F32))


def downward(
    count, inc0, near_base, own1, own2, own3, x_even, x_odd, rad, rec, near, ts, shf,
    field, xlo, xhi, hc, hx, tot, inc1, inc2, inc3, half,
):
    received("row", x_even, x_odd, xlo, xhi)
    sides = []
    for s, src in enumerate((xlo, xhi)):
        for xr in range(2):
            sides.append(jnp.concatenate([src[4 * xr + c, 0:32, :] for c in range(4)], axis=1))
        for c in range(4):
            hc[s, c, 0:24, :] = src[4 * (1 - s) + c, 0:24, :]
    halo = jnp.dot(jnp.concatenate(sides, axis=0).astype(BF16), rad[...], preferred_element_type=F32)
    halo = halo.astype(BF16).astype(F32)
    for c in range(4):
        re, im = halo[:, lanes(c)], halo[:, lanes(4 + c)]
        for q, part in enumerate((re, im, re + im)):
            hx[4 * q + c] = part

    for c in range(8):
        for x in range(2):
            at = slice(x * 8, x * 8 + 2)
            both = slice(20 + 2 * x, 22 + 2 * x)
            inc3[c, at, :] = own3[c, at, :] + xlo[c, both, :] + xhi[c, both, :]
        for x in range(4):
            at = slice(x * 8, x * 8 + 4)
            side = (xlo, xhi)[x // 2]
            inc2[c, at, :] = own2[c, at, :] + side[c, 24 + 4 * (x % 2) : 28 + 4 * (x % 2), :]
        for x in range(8):
            at = slice(x * 8, x * 8 + 8)
            value = own1[c, at, :]
            if x in (0, 1, 6, 7):
                value = value + (xlo, xhi)[x // 6][c, 32 + 8 * (x % 2) : 40 + 8 * (x % 2), :]
            inc1[c, at, :] = value
    add_parent(inc2, inc3, shf, 2, 4)
    add_parent(inc1, inc2, shf, 1, 8)

    def leaf_columns(x):
        for b in range(2):
            row = slice(2 * (x % 2) + b, 2 * (x % 2) + b + 1)
            at = pl.ds(x * 16 + b, 8, stride=2)
            for c in range(4):
                q_re = inc1[c, (x // 2) * 8 : (x // 2) * 8 + 8, :]
                q_im = inc1[4 + c, (x // 2) * 8 : (x // 2) * 8 + 8, :]
                t_re = shf[0, row, lanes(c)]
                t_im = shf[0, row, lanes(4 + c)]
                tot[c, at, :] = inc0[c, at, :] + (t_re * q_re + t_im * q_im)
                tot[4 + c, at, :] = inc0[4 + c, at, :] + (t_re * q_im - t_im * q_re)

    def from_x_halo(s):
        for c in range(4):
            acc = {}
            for xr in range(2):
                xs = 4 * s + xr
                for k in range(6):
                    value = values(hx, c, pl.ds((2 * s + xr) * 32 + k, 8, stride=2))
                    for a in range(2):
                        for b in range(2):
                            dx, dy = xs - 2 - a, k - 2 - b
                            if far(dx, dy):
                                acc[a, b] = add_product(acc.get((a, b)), factors(ts, 0, dx, dy, c), value)
            for (a, b), sums in acc.items():
                at = pl.ds((14 * s + a) * 16 + b, 8, stride=2)
                for q, total in enumerate(complex_sum(sums)):
                    tot[4 * q + c, at, :] = tot[4 * q + c, at, :] + total

    def near_side(s):
        total = None
        for dy in range(3):
            rows = jnp.concatenate([hc[s, c, 1 + dy : 17 + dy, :] for c in range(4)], axis=1).astype(BF16)
            term = jnp.dot(rows, near[6 * s + dy], preferred_element_type=F32)
            total = term if total is None else total + term
        return total

    for x in range(N0):
        leaf_columns(x)
    for s in range(2):
        from_x_halo(s)
    for c in range(8):
        half[:, lanes(c)] = tot[c].astype(BF16)
    sides = [near_side(s) for s in range(2)]
    total = jnp.dot(half[...], rec[...], preferred_element_type=F32)
    for x in range(N0):
        own = slice(x * 16, x * 16 + 16)
        for c in range(4):
            result = total[own, lanes(c)] + near_base[c, own, :]
            if x in (0, N0 - 1):
                result = result + sides[x // (N0 - 1)][:, lanes(c)]
            field[x, :, lanes(c)] = jnp.where(occupied(count[own, :], c), result, 0.0).astype(BF16)


def call(kernel, outs, scratch, flops, *args, aliases=None):
    place = pl.BlockSpec(memory_space=pltpu.VMEM)
    return pl.pallas_call(
        kernel,
        out_shape=outs,
        in_specs=[place] * len(args),
        out_specs=[place] * len(outs),
        input_output_aliases=aliases or {},
        scratch_shapes=scratch,
        compiler_params=pltpu.CompilerParams(vmem_limit_bytes=16 * 1024 * 1024),
        cost_estimate=pl.CostEstimate(flops=flops, bytes_accessed=1 << 20, transcendentals=0),
        interpret=INTERPRET,
    )(*args)


def shape(dims, kind):
    return jax.ShapeDtypeStruct(dims, kind)


def swap(value, axis, odd):
    return lax.ppermute(value, ("row", "col"), swap_perm(axis, odd))


def shards(currents, counts, radiate, receive, near_blocks, translate, shift):
    mem = pltpu.VMEM
    factor = jnp.transpose(translate, (1, 0, 2))
    ys, xs, strip = mem((8, SY, 128), F32), mem((8, MX, 128), F32), mem((8, SX, 128), F32)
    (f0,) = call(opening, [shape((12, 20 * ROW0, 128), F32)], [], 10**13)
    masked, c0, count = call(
        mask,
        [shape((16, 16, 512), BF16), shape((4, 256, 128), F32), shape((256, 128), F32)],
        [],
        1,
        currents, counts,
    )
    f0, p1, p2, p3, m_odd, m_even = call(
        upward,
        [
            shape((12, 20 * ROW0, 128), F32),
            shape((8, 64, 128), F32),
            shape((8, 32, 128), F32),
            shape((8, 16, 128), F32),
            shape((8, SY, 128), BF16),
            shape((8, SY, 128), BF16),
        ],
        [ys, ys],
        10**12,
        f0, masked, c0, radiate, shift,
        aliases={0: 0},
    )
    r_odd = swap(m_odd, "col", 1)
    r_even = swap(m_even, "col", 0)
    inc0, sums, t_rr, t_ii = call(
        inside,
        [
            shape((8, 32 * FIRST, 128), F32), shape((49, 4, 1536), F32),
            shape((784, 128), F32), shape((784, 128), F32),
        ],
        [],
        4 * 10**9,
        f0, factor,
    )
    r_odd, r_even, inc0 = lax.optimization_barrier((r_odd, r_even, inc0))
    s_even, s_odd = call(
        strips,
        [shape((8, MX, 128), BF16)] * 2,
        [
            ys, ys, strip, strip, mem((12, 48, 128), F32), xs, xs,
            mem((512, 128), F32), mem((512, 128), F32), mem((128, 128), F32),
            mem((288, 128), F32), mem((288, 128), F32), mem((32, 128), F32),
            mem((288, 128), F32), mem((288, 128), F32), mem((32, 128), F32),
        ],
        10**7,
        r_odd, r_even, masked, p1, p2, p3, sums, t_rr, t_ii,
    )
    x_even = swap(s_even, "row", 0)
    x_odd = swap(s_odd, "row", 1)
    inc0, near_sum, own1, own2, own3 = call(
        beside_y,
        [
            shape((8, 256, 128), F32), shape((4, 256, 128), F32),
            shape((8, 64, 128), F32), shape((8, 32, 128), F32), shape((8, 16, 128), F32),
        ],
        [
            ys, ys, mem((12, 128, 128), F32), mem((8, 8 * ROWS, 128), F32), mem((3, 12, 128, 128), F32),
            mem((512, 128), F32), mem((512, 128), F32), mem((128, 128), F32),
            mem((288, 128), F32), mem((288, 128), F32), mem((32, 128), F32),
            mem((4, 16 * ROW0, 128), F32), mem((18, 16, 1536), BF16),
        ],
        10**9,
        r_odd, r_even, masked, f0, p1, p2, p3, inc0, radiate, near_blocks, sums, t_rr, t_ii,
    )
    (field,) = call(
        downward,
        [shape((16, 16, 512), BF16)],
        [
            xs, xs, mem((2, 4, 24, 128), F32), mem((12, 128, 128), F32),
            mem((8, 256, 128), F32), mem((8, 64, 128), F32), mem((8, 32, 128), F32), mem((8, 16, 128), F32),
            mem((256, 1024), BF16),
        ],
        3 * 10**9,
        count, inc0, near_sum, own1, own2, own3, x_even, x_odd,
        radiate, receive, near_blocks, sums, shift,
    )
    return field


def solution(mesh):
    return jax.shard_map(
        shards,
        mesh=mesh,
        in_specs=(P("row", "col", None), P("row", "col"), P(), P(), P(), P(), P()),
        out_specs=P("row", "col", None),
        check_vma=False,
    )
```

```python
import jax
import jax.numpy as jnp
from jax import lax
from jax.experimental import pallas as pl
from jax.experimental.pallas import tpu as pltpu
from jax.sharding import PartitionSpec as P

U = 16
INTERPRET = False
F32 = jnp.float32
BF16 = jnp.bfloat16
N0 = 16
ROW0 = 32
ROWS = 24
SX = 72
MX = 48
SY = 48
FIRST = 7


def far(dx, dy):
    return max(abs(dx), abs(dy)) >= 2 and max(abs(dx), abs(dy)) <= 3


def lanes(c):
    return slice(c * 128, (c + 1) * 128)


def factors(ts, level, dx, dy, c):
    row = (dx + 3) * 7 + dy + 3
    return [ts[row, level : level + 1, lanes(4 * n + c)] for n in range(3)]


def values(ref, c, at):
    return [ref[4 * n + c, at, :] for n in range(3)]


def count_rows(cnt_ref, x):
    row = cnt_ref[x : x + 1, :].astype(F32)
    one = lax.broadcasted_iota(jnp.int32, (N0, N0), 0) == lax.broadcasted_iota(jnp.int32, (N0, N0), 1)
    return jnp.sum(jnp.where(one, jnp.broadcast_to(row, (N0, N0)), 0.0), axis=1, keepdims=True)


def occupied(count, c):
    lane = lax.broadcasted_iota(jnp.int32, count.shape, 1).astype(F32) + float(128 * c)
    return lane < count * float(2 * U)


def swap_perm(axis, odd):
    size = (lax.axis_size("row"), lax.axis_size("col"))
    which = ("row", "col").index(axis)
    perm = []
    for row in range(size[0]):
        for col in range(size[1]):
            at = [row, col]
            to = at[which] + (1 if at[which] % 2 == odd else -1)
            if 0 <= to < size[which]:
                at[which] = to
            else:
                at[1 - which] ^= 1
            perm.append((row * size[1] + col, at[0] * size[1] + at[1]))
    return perm


def add_product(acc, factor, value):
    terms = (factor[0] * value[2], factor[1] * value[0], factor[2] * value[1])
    return terms if acc is None else tuple(old + term for old, term in zip(acc, terms))


def complex_sum(acc):
    return acc[0] - acc[2], acc[0] + acc[1]


def opening(f0):
    zero = jnp.zeros((8, 128), F32)
    for c in range(12):
        for x in range(N0):
            base = (x + 2) * ROW0
            f0[c, base : base + 8, :] = zero
            f0[c, base + 24 : base + 32, :] = zero


def mask(cur, cnt, msk, c0, count):
    for x in range(N0):
        here = slice(x * 16, (x + 1) * 16)
        count[here, :] = jnp.broadcast_to(count_rows(cnt, x), (N0, 128))
        for c in range(4):
            kept = jnp.where(occupied(count[here, :], c), cur[x, :, lanes(c)].astype(F32), 0.0)
            msk[x, :, lanes(c)] = kept.astype(BF16)
            c0[c, here, :] = kept


def upward(f0_zero, msk, c0, rad, shf, f0, p1, p2, p3, m_odd, m_even, me, mo):
    even = (lax.axis_index("col") % 2) == 0
    lhs = msk[...].reshape(N0 * N0, 512)
    for m in range(2):
        re, im = [
            jnp.dot(lhs, rad[:, n : n + 256], preferred_element_type=F32).astype(BF16).astype(F32)
            for n in (256 * m, 512 + 256 * m)
        ]
        for n, out in enumerate((re, im)):
            for h in range(2):
                for x in range(N0):
                    base = (x + 2) * ROW0
                    c = 4 * n + 2 * m + h
                    f0[c, base + 8 : base + 24, :] = out[x * 16 : (x + 1) * 16, lanes(h)]
    for level, (dest, size) in enumerate(((p1, 8), (p2, 4), (p3, 2))):
        for i in range(size):
            for c in range(4):
                acc = None
                for a in range(2):
                    for b in range(2):
                        if level == 0:
                            at = pl.ds((2 * i + a + 2) * ROW0 + 8 + b, size, stride=2)
                            value = (f0[c, at, :], f0[4 + c, at, :])
                        else:
                            at = pl.ds((2 * i + a) * 8 + b, size, stride=2)
                            value = ((p1, p2)[level - 1][c, at, :], (p1, p2)[level - 1][4 + c, at, :])
                        row = slice(2 * a + b, 2 * a + b + 1)
                        t_re, t_im = shf[level, row, lanes(c)], shf[level, row, lanes(4 + c)]
                        re = t_re * value[0] - t_im * value[1]
                        im = t_re * value[1] + t_im * value[0]
                        acc = (re, im) if acc is None else (acc[0] + re, acc[1] + im)
                dest[c, i * 8 : i * 8 + size, :] = acc[0].astype(BF16).astype(F32)
                dest[4 + c, i * 8 : i * 8 + size, :] = acc[1].astype(BF16).astype(F32)

    def put(c, at, lo, hi):
        me[c, at, :] = jnp.where(even, hi, lo)
        mo[c, at, :] = jnp.where(even, lo, hi)

    for r in range(2):
        for c in range(4):
            lo = c0[c, pl.ds(r, 16, stride=16), :]
            hi = c0[c, pl.ds(14 + r, 16, stride=16), :]
            for h in range(2):
                put(c + 4 * h, pl.ds(r, 8, stride=2), lo[8 * h : 8 * h + 8], hi[8 * h : 8 * h + 8])
        for c in range(8):
            put(c, pl.ds(16 + r, 8, stride=2), p1[c, pl.ds(r, 8, stride=8), :], p1[c, pl.ds(6 + r, 8, stride=8), :])
            put(c, pl.ds(32 + r, 4, stride=2), p2[c, pl.ds(r, 4, stride=8), :], p2[c, pl.ds(2 + r, 4, stride=8), :])
            both = p3[c, pl.ds(r, 2, stride=8), :]
            put(c, pl.ds(40 + r, 2, stride=2), both, both)
    for c in range(8):
        me[c, 44:48, :] = jnp.zeros((4, 128), F32)
        mo[c, 44:48, :] = jnp.zeros((4, 128), F32)
        m_even[c] = me[c].astype(BF16)
        m_odd[c] = mo[c].astype(BF16)


def leaf(f0, ts, inc, i):
    for c in range(4):
        acc = {}
        for xs in range(6):
            if not 0 <= 2 * i + xs - 2 < N0:
                continue
            for k in range(6):
                if xs in (2, 3) and k in (2, 3):
                    continue
                value = values(f0, c, pl.ds((2 * i + xs) * ROW0 + 6 + k, 8, stride=2))
                for a in range(2):
                    for b in range(2):
                        dx, dy = xs - 2 - a, k - 2 - b
                        if far(dx, dy):
                            acc[a, b] = add_product(acc.get((a, b)), factors(ts, 0, dx, dy, c), value)
        for (a, b), sums in acc.items():
            for q, total in enumerate(complex_sum(sums)):
                inc[4 * q + c, pl.ds((2 * i + a) * 16 + b, 8, stride=2), :] = total


def inside(f0_in, tr, f0, inc, ts, t_rr, t_ii):
    re, im = tr[:, :, 0:512], tr[:, :, 512:1024]
    ts[:, :, 0:512] = re
    ts[:, :, 512:1024] = im - re
    ts[:, :, 1024:1536] = re + im
    for c in range(4):
        for x in range(N0):
            own = slice((x + 2) * ROW0 + 8, (x + 2) * ROW0 + 24)
            f0[8 + c, own, :] = f0[c, own, :] + f0[4 + c, own, :]
    offsets = [(dx, dy) for dx in range(-3, 4) for dy in range(-3, 4) if far(dx, dy)]
    for i in range(FIRST):
        leaf(f0, ts, inc, i)
        for dx, dy in offsets[i::FIRST]:
            row = (dx + 3) * 7 + dy + 3
            for c in range(4):
                re = tr[row, 2:4, lanes(c)]
                im = tr[row, 2:4, lanes(4 + c)]
                t_rr[pl.ds(row * 8 + c, 2, stride=392), :] = re
                t_rr[pl.ds(row * 8 + 4 + c, 2, stride=392), :] = re
                t_ii[pl.ds(row * 8 + c, 2, stride=392), :] = -im
                t_ii[pl.ds(row * 8 + 4 + c, 2, stride=392), :] = im


def received(axis, r_even, r_odd, lo, hi):
    me = lax.axis_index(axis)
    last = lax.axis_size(axis) - 1
    even = (me % 2) == 0
    for c in range(8):
        from_even = r_even[c].astype(F32)
        from_odd = r_odd[c].astype(F32)
        lo[c] = jnp.where(me == 0, 0.0, jnp.where(even, from_odd, from_even))
        hi[c] = jnp.where(me == last, 0.0, jnp.where(even, from_even, from_odd))


def strips(
    r_odd, r_even, msk, p1, p2, p3, ts, t_rr, t_ii, x_even, x_odd,
    ylo, yhi, mlo, mhi, xs1, left, right, box2, swp2, out2, box3, swp3, out3, box4, swp4, out4,
):
    received("col", r_even, r_odd, ylo, yhi)
    even = (lax.axis_index("row") % 2) == 0
    for dest, first in ((mlo, 0), (mhi, 1)):
        for xr in range(2):
            x = 14 * first + xr
            kept = msk[x].astype(F32)
            for c in range(4):
                dest[4 * xr + c, 2:18, :] = kept[:, lanes(c)]
                at = slice(2 * (x % 8), 2 * (x % 8) + 2)
                dest[4 * xr + c, 0:2, :] = ylo[c + 4 * (x // 8), at, :]
                dest[4 * xr + c, 18:20, :] = yhi[c + 4 * (x // 8), at, :]
            for c in range(8):
                for level_ref, size, base, within in ((p1, 8, 32, 16), (p2, 4, 56, 32), (p3, 2, 20, 40)):
                    x = (size - 2) * first + xr
                    at = base + (size + 4) * xr
                    dest[c, at + 2 : at + 2 + size, :] = level_ref[c, x * 8 : x * 8 + size, :]
                    dest[c, at : at + 2, :] = ylo[c, within + 2 * x : within + 2 * x + 2, :]
                    dest[c, at + 2 + size : at + 4 + size, :] = yhi[c, within + 2 * x : within + 2 * x + 2, :]
    both = ((right, mhi), (left, mlo))
    for c in range(4):
        for s, (_, src) in enumerate(both):
            re, im = src[c, 32:56, :], src[4 + c, 32:56, :]
            for q, part in enumerate((re, im, re + im)):
                xs1[4 * q + c, s * 24 : s * 24 + 24, :] = part
    for s, (message, src) in enumerate(both):
        for c in range(8):
            message[c, 0:20, :] = src[c, 0:20, :]
        for c in range(4):
            acc = {}
            for xr in range(2):
                xs = 4 * s + xr
                for k in range(6):
                    value = values(xs1, c, pl.ds((2 * s + xr) * 12 + k, 4, stride=2))
                    for a in range(2):
                        for b in range(2):
                            dx, dy = xs - 2 - a, k - 2 - b
                            if far(dx, dy):
                                acc[a, b] = add_product(acc.get((a, b)), factors(ts, 1, dx, dy, c), value)
            for (a, b), sums in acc.items():
                for q, total in enumerate(complex_sum(sums)):
                    message[4 * q + c, pl.ds(32 + 8 * a + b, 4, stride=2), :] = total
    rows = [(6 * s + xr, [(0, 8, src, 56 + 8 * xr)]) for s, (_, src) in enumerate(both) for xr in range(2)]
    by_box(2, 4, rows, t_rr, t_ii, box2, swp2, out2)
    for s, (message, src) in enumerate(both):
        box, swapped, out = ((box3, swp3, out3), (box4, swp4, out4))[s]
        by_box(3, 2, [(4 * s + xr, [(0, 6, src, 20 + 6 * xr)]) for xr in range(2)], t_rr, t_ii, box, swapped, out)
        for c in range(8):
            message[c, 20:24, :] = out[pl.ds(c, 4, stride=8), :]
            for a in range(2):
                message[c, 24 + 4 * a : 28 + 4 * a, :] = out2[pl.ds((2 * s + a) * 32 + c, 4, stride=8), :]
    for c in range(8):
        lo = left[c]
        hi = right[c]
        x_even[c] = jnp.where(even, hi, lo).astype(BF16)
        x_odd[c] = jnp.where(even, lo, hi).astype(BF16)


def beside_y(
    r_odd, r_even, msk, f0, p1, p2, p3, inc0, rad, near, ts, t_rr, t_ii, base0, near_base, own1, own2, own3,
    ylo, yhi, hy, f1, g1, box2, swp2, out2, box3, swp3, out3, cx, ln,
):
    received("col", r_even, r_odd, ylo, yhi)
    blocks = []
    zero = jnp.zeros((8, 128), F32)
    for x in range(N0):
        kept = msk[x].astype(F32)
        for c in range(4):
            cx[c, x * ROW0 + 8 : x * ROW0 + 24, :] = kept[:, lanes(c)]
    for s, src in enumerate((ylo, yhi)):
        for r in range(2):
            both = [
                jnp.concatenate([src[4 * h + c, pl.ds(r, 8, stride=2), :] for c in range(4)], axis=1) for h in range(2)
            ]
            blocks.append(jnp.concatenate(both, axis=0))
        touching = blocks[2 * s + 1 - s]
        for c in range(4):
            cx[c, pl.ds(7 + 17 * s, 16, stride=ROW0), :] = touching[:, lanes(c)]
    halo = jnp.dot(jnp.concatenate(blocks, axis=0).astype(BF16), rad[...], preferred_element_type=F32)
    halo = halo.astype(BF16).astype(F32)
    for c in range(4):
        re, im = halo[:, lanes(c)], halo[:, lanes(4 + c)]
        for q, part in enumerate((re, im, re + im)):
            for n in range(4):
                hy[4 * q + c, n * 32 : n * 32 + 8, :] = zero
                hy[4 * q + c, n * 32 + 8 : n * 32 + 24, :] = part[16 * n : 16 * n + 16]
                hy[4 * q + c, n * 32 + 24 : n * 32 + 32, :] = zero
    ln[0] = jnp.zeros((16, 1536), BF16)
    ln[17] = jnp.zeros((16, 1536), BF16)
    for dy in range(3):
        for x in range(N0):
            for c in range(4):
                at = x * ROW0 + 7 + dy
                ln[x + 1, :, lanes(4 * dy + c)] = cx[c, at : at + 16, :].astype(BF16)
    for c in range(8):
        for x in range(8):
            base = x * ROWS
            f1[c, base + 8 : base + 16, :] = p1[c, x * 8 : x * 8 + 8, :]
            f1[c, base + 6 : base + 8, :] = ylo[c, 16 + 2 * x : 18 + 2 * x, :]
            f1[c, base + 16 : base + 18, :] = yhi[c, 16 + 2 * x : 18 + 2 * x, :]
    for c in range(4):
        for s in range(3):
            for xe in range(8):
                for h in range(2):
                    x = xe + 4 * h - 2
                    at = slice(xe * 16 + 8 * h, xe * 16 + 8 * h + 8)
                    if 0 <= x < 8:
                        base = x * ROWS + 6 + 2 * s
                        re, im = f1[c, base : base + 8, :], f1[4 + c, base : base + 8, :]
                        parts = (re, im, re + im)
                    else:
                        parts = (zero, zero, zero)
                    for q, part in enumerate(parts):
                        g1[s, 4 * q + c, at, :] = part
    for c in range(8):
        base0[c, 0 : FIRST * 32, :] = inc0[c]

    def near_term(n):
        dx, h = n % 3, n // 3
        rows = ln[dx : dx + 16].reshape(N0 * N0, 1536)
        weights = near[3 * dx : 3 * dx + 3, :, h * 256 : h * 256 + 256].reshape(1536, 256)
        term = jnp.dot(rows, weights, preferred_element_type=F32)
        for q in range(2):
            if dx == 0:
                near_base[2 * h + q] = term[:, lanes(q)]
            else:
                near_base[2 * h + q] = near_base[2 * h + q] + term[:, lanes(q)]

    def across_y(s, c):
        acc = {}
        for r in range(2):
            for xs in range(6):
                value = values(hy, c, pl.ds((2 * s + r) * 32 + 6 + xs, 8, stride=2))
                for a in range(2):
                    for b in range(2):
                        dx, dy = xs - 2 - a, 4 * s - 2 + r - b
                        if far(dx, dy):
                            acc[a, b] = add_product(acc.get((a, b)), factors(ts, 0, dx, dy, c), value)
        for (a, b), sums in acc.items():
            for q, total in enumerate(complex_sum(sums)):
                at = pl.ds(16 * a + 14 * s + b, 8, stride=32)
                base0[4 * q + c, at, :] = base0[4 * q + c, at, :] + total

    def middle(i, c):
        acc = {}
        for xs in range(6):
            for k in range(6):
                if xs in (2, 3) and k in (2, 3):
                    continue
                at = pl.ds((2 * i + xs) * 16 + k % 2, 8, stride=2)
                value = [g1[k // 2, 4 * q + c, at, :] for q in range(3)]
                for a in range(2):
                    for b in range(2):
                        dx, dy = xs - 2 - a, k - 2 - b
                        if far(dx, dy):
                            acc[a, b] = add_product(acc.get((a, b)), factors(ts, 1, dx, dy, c), value)
        for (a, b), sums in acc.items():
            for q, total in enumerate(complex_sum(sums)):
                for h in range(2):
                    at = pl.ds((2 * (i + 2 * h) + a) * 8 + b, 4, stride=2)
                    own1[4 * q + c, at, :] = total[4 * h : 4 * h + 4]

    def small(level):
        size, own, base, inc = {2: (4, p2, 32, own2), 3: (2, p3, 40, own3)}[level]
        box, swapped, out = {2: (box2, swp2, out2), 3: (box3, swp3, out3)}[level]
        rows = [
            (x + 2, [(2, size, own, x * 8), (0, 2, ylo, base + 2 * x), (size + 2, 2, yhi, base + 2 * x)])
            for x in range(size)
        ]
        by_box(level, size, rows, t_rr, t_ii, box, swapped, out)
        for c in range(8):
            for x in range(size):
                inc[c, x * 8 : x * 8 + size, :] = out[pl.ds(x * size * 8 + c, size, stride=8), :]

    for n in range(6):
        near_term(n)
        if n < 4:
            for i in range(2):
                middle(i, n)
        else:
            for c in range(4):
                across_y(n - 4, c)
        if n in (1, 2):
            small(n + 1)
        if n == 3:
            for i in range(FIRST, 8):
                leaf(f0, ts, base0, i)


def add_parent(inc, parent, shf, level, size):
    half = size // 2
    for x in range(size):
        for b in range(2):
            row = slice(2 * (x % 2) + b, 2 * (x % 2) + b + 1)
            at = pl.ds(x * 8 + b, half, stride=2)
            for c in range(4):
                q_re = parent[c, (x // 2) * 8 : (x // 2) * 8 + half, :]
                q_im = parent[4 + c, (x // 2) * 8 : (x // 2) * 8 + half, :]
                t_re = shf[level, row, lanes(c)]
                t_im = shf[level, row, lanes(4 + c)]
                inc[c, at, :] = inc[c, at, :] + (t_re * q_re + t_im * q_im)
                inc[4 + c, at, :] = inc[4 + c, at, :] + (t_re * q_im - t_im * q_re)


def by_box(level, size, rows, t_rr, t_ii, box, swapped, out):
    wide = size + 4
    for c in range(8):
        for xe, pieces in rows:
            for ye, count, src, at in pieces:
                piece = src[c, at : at + count, :]
                first = (xe * wide + ye) * 8
                box[pl.ds(first + c, count, stride=8), :] = piece
                swapped[pl.ds(first + (c + 4) % 8, count, stride=8), :] = piece
    given = [xe for xe, _ in rows]
    for i in range(size // 2):
        for j in range(size // 2):
            acc = {}
            for xs in range(6):
                if 2 * i + xs not in given:
                    continue
                for k in range(6):
                    if xs in (2, 3) and k in (2, 3):
                        continue
                    at = ((2 * i + xs) * wide + 2 * j + k) * 8
                    value = box[at : at + 8, :]
                    other = swapped[at : at + 8, :]
                    for a in range(2):
                        for b in range(2):
                            dx, dy = xs - 2 - a, k - 2 - b
                            if far(dx, dy):
                                row = (level - 2) * 392 + ((dx + 3) * 7 + dy + 3) * 8
                                term = t_rr[row : row + 8, :] * value + t_ii[row : row + 8, :] * other
                                acc[a, b] = term if (a, b) not in acc else acc[a, b] + term
            for a in range(2):
                for b in range(2):
                    at = ((2 * i + a) * size + 2 * j + b) * 8
                    out[at : at + 8, :] = acc.get((a, b), jnp.zeros((8, 128), F32))


def downward(
    count, inc0, near_base, own1, own2, own3, x_even, x_odd, rad, rec, near, ts, shf,
    field, xlo, xhi, hc, hx, tot, inc1, inc2, inc3, half,
):
    received("row", x_even, x_odd, xlo, xhi)
    sides = []
    for s, src in enumerate((xlo, xhi)):
        for xr in range(2):
            sides.append(jnp.concatenate([src[4 * xr + c, 0:24, :] for c in range(4)], axis=1))
        for c in range(4):
            hc[s, c, 0:24, :] = src[4 * (1 - s) + c, 0:24, :]
    halo = jnp.dot(jnp.concatenate(sides, axis=0).astype(BF16), rad[...], preferred_element_type=F32)
    halo = halo.astype(BF16).astype(F32)
    for c in range(4):
        re, im = halo[:, lanes(c)], halo[:, lanes(4 + c)]
        for q, part in enumerate((re, im, re + im)):
            hx[4 * q + c] = part

    for c in range(8):
        for x in range(2):
            at = slice(x * 8, x * 8 + 2)
            both = slice(20 + 2 * x, 22 + 2 * x)
            inc3[c, at, :] = own3[c, at, :] + xlo[c, both, :] + xhi[c, both, :]
        for x in range(4):
            at = slice(x * 8, x * 8 + 4)
            side = (xlo, xhi)[x // 2]
            inc2[c, at, :] = own2[c, at, :] + side[c, 24 + 4 * (x % 2) : 28 + 4 * (x % 2), :]
        for x in range(8):
            at = slice(x * 8, x * 8 + 8)
            value = own1[c, at, :]
            if x in (0, 1, 6, 7):
                value = value + (xlo, xhi)[x // 6][c, 32 + 8 * (x % 2) : 40 + 8 * (x % 2), :]
            inc1[c, at, :] = value
    add_parent(inc2, inc3, shf, 2, 4)
    add_parent(inc1, inc2, shf, 1, 8)

    def leaf_columns(x):
        for b in range(2):
            row = slice(2 * (x % 2) + b, 2 * (x % 2) + b + 1)
            at = pl.ds(x * 16 + b, 8, stride=2)
            for c in range(4):
                q_re = inc1[c, (x // 2) * 8 : (x // 2) * 8 + 8, :]
                q_im = inc1[4 + c, (x // 2) * 8 : (x // 2) * 8 + 8, :]
                t_re = shf[0, row, lanes(c)]
                t_im = shf[0, row, lanes(4 + c)]
                tot[c, at, :] = inc0[c, at, :] + (t_re * q_re + t_im * q_im)
                tot[4 + c, at, :] = inc0[4 + c, at, :] + (t_re * q_im - t_im * q_re)

    def from_x_halo(s):
        for c in range(4):
            acc = {}
            for xr in range(2):
                xs = 4 * s + xr
                for k in range(6):
                    value = values(hx, c, pl.ds((2 * s + xr) * 24 + k, 8, stride=2))
                    for a in range(2):
                        for b in range(2):
                            dx, dy = xs - 2 - a, k - 2 - b
                            if far(dx, dy):
                                acc[a, b] = add_product(acc.get((a, b)), factors(ts, 0, dx, dy, c), value)
            for (a, b), sums in acc.items():
                at = pl.ds((14 * s + a) * 16 + b, 8, stride=2)
                for q, total in enumerate(complex_sum(sums)):
                    tot[4 * q + c, at, :] = tot[4 * q + c, at, :] + total

    def near_side(s):
        total = None
        for dy in range(3):
            rows = jnp.concatenate([hc[s, c, 1 + dy : 17 + dy, :] for c in range(4)], axis=1).astype(BF16)
            term = jnp.dot(rows, near[6 * s + dy], preferred_element_type=F32)
            total = term if total is None else total + term
        return total

    for x in range(N0):
        leaf_columns(x)
    for s in range(2):
        from_x_halo(s)
    for c in range(8):
        half[:, lanes(c)] = tot[c].astype(BF16)
    sides = [near_side(s) for s in range(2)]
    total = jnp.dot(half[...], rec[...], preferred_element_type=F32)
    for x in range(N0):
        own = slice(x * 16, x * 16 + 16)
        for c in range(4):
            result = total[own, lanes(c)] + near_base[c, own, :]
            if x in (0, N0 - 1):
                result = result + sides[x // (N0 - 1)][:, lanes(c)]
            field[x, :, lanes(c)] = jnp.where(occupied(count[own, :], c), result, 0.0).astype(BF16)


def call(kernel, outs, scratch, flops, *args, aliases=None):
    place = pl.BlockSpec(memory_space=pltpu.VMEM)
    return pl.pallas_call(
        kernel,
        out_shape=outs,
        in_specs=[place] * len(args),
        out_specs=[place] * len(outs),
        input_output_aliases=aliases or {},
        scratch_shapes=scratch,
        compiler_params=pltpu.CompilerParams(vmem_limit_bytes=16 * 1024 * 1024),
        cost_estimate=pl.CostEstimate(flops=flops, bytes_accessed=1 << 20, transcendentals=0),
        interpret=INTERPRET,
    )(*args)


def shape(dims, kind):
    return jax.ShapeDtypeStruct(dims, kind)


def swap(value, axis, odd):
    return lax.ppermute(value, ("row", "col"), swap_perm(axis, odd))


def shards(currents, counts, radiate, receive, near_blocks, translate, shift):
    mem = pltpu.VMEM
    factor = jnp.transpose(translate, (1, 0, 2))
    ys, xs, strip = mem((8, SY, 128), F32), mem((8, MX, 128), F32), mem((8, SX, 128), F32)
    (f0,) = call(opening, [shape((12, 20 * ROW0, 128), F32)], [], 10**13)
    masked, c0, count = call(
        mask,
        [shape((16, 16, 512), BF16), shape((4, 256, 128), F32), shape((256, 128), F32)],
        [],
        1,
        currents, counts,
    )
    f0, p1, p2, p3, m_odd, m_even = call(
        upward,
        [
            shape((12, 20 * ROW0, 128), F32),
            shape((8, 64, 128), F32),
            shape((8, 32, 128), F32),
            shape((8, 16, 128), F32),
            shape((8, SY, 128), BF16),
            shape((8, SY, 128), BF16),
        ],
        [ys, ys],
        10**12,
        f0, masked, c0, radiate, shift,
        aliases={0: 0},
    )
    r_odd = swap(m_odd, "col", 1)
    r_even = swap(m_even, "col", 0)
    f0, inc0, sums, t_rr, t_ii = call(
        inside,
        [
            shape((12, 20 * ROW0, 128), F32),
            shape((8, 32 * FIRST, 128), F32), shape((49, 4, 1536), F32),
            shape((784, 128), F32), shape((784, 128), F32),
        ],
        [],
        4 * 10**9,
        f0, factor,
        aliases={0: 0},
    )
    r_odd, r_even, inc0 = lax.optimization_barrier((r_odd, r_even, inc0))
    s_even, s_odd = call(
        strips,
        [shape((8, MX, 128), BF16)] * 2,
        [
            ys, ys, strip, strip, mem((12, 48, 128), F32), xs, xs,
            mem((512, 128), F32), mem((512, 128), F32), mem((128, 128), F32),
            mem((288, 128), F32), mem((288, 128), F32), mem((32, 128), F32),
            mem((288, 128), F32), mem((288, 128), F32), mem((32, 128), F32),
        ],
        10**7,
        r_odd, r_even, masked, p1, p2, p3, sums, t_rr, t_ii,
    )
    x_even = swap(s_even, "row", 0)
    x_odd = swap(s_odd, "row", 1)
    inc0, near_sum, own1, own2, own3 = call(
        beside_y,
        [
            shape((8, 256, 128), F32), shape((4, 256, 128), F32),
            shape((8, 64, 128), F32), shape((8, 32, 128), F32), shape((8, 16, 128), F32),
        ],
        [
            ys, ys, mem((12, 128, 128), F32), mem((8, 8 * ROWS, 128), F32), mem((3, 12, 128, 128), F32),
            mem((512, 128), F32), mem((512, 128), F32), mem((128, 128), F32),
            mem((288, 128), F32), mem((288, 128), F32), mem((32, 128), F32),
            mem((4, 16 * ROW0, 128), F32), mem((18, 16, 1536), BF16),
        ],
        10**9,
        r_odd, r_even, masked, f0, p1, p2, p3, inc0, radiate, near_blocks, sums, t_rr, t_ii,
    )
    (field,) = call(
        downward,
        [shape((16, 16, 512), BF16)],
        [
            xs, xs, mem((2, 4, 24, 128), F32), mem((12, 96, 128), F32),
            mem((8, 256, 128), F32), mem((8, 64, 128), F32), mem((8, 32, 128), F32), mem((8, 16, 128), F32),
            mem((256, 1024), BF16),
        ],
        3 * 10**9,
        count, inc0, near_sum, own1, own2, own3, x_even, x_odd,
        radiate, receive, near_blocks, sums, shift,
    )
    return field


def solution(mesh):
    return jax.shard_map(
        shards,
        mesh=mesh,
        in_specs=(P("row", "col", None), P("row", "col"), P(), P(), P(), P(), P()),
        out_specs=P("row", "col", None),
        check_vma=False,
    )
```
